512 devices in a mesh: seq: 32 (over y, x), head: 2 (over core), expert: 8 (over z).
Axes of the slice: x: 4, y: 8, z: 8, core: 2. Of those that a mesh axis runs over, the one named last changes fastest.
Arguments:
- query_proj: bfloat16 [8, 4096, 2048], P('expert', 'seq', 'head'), may hold values from -6 to 6
- key_proj: bfloat16 [8, 4096, 2048], P('expert', 'seq', 'head'), may hold values from -6 to 6
- value_proj: bfloat16 [8, 4096, 2048], P('expert', 'seq', 'head'), may hold values from -6 to 6
- init_state: float32 [8, 16, 128, 128], P('expert', 'head'), may hold values from -384 to 384
- residual: bfloat16 [8, 4096, 2048], P('expert', ('seq', 'head')), may hold values from -6 to 6
- out_gain: float32 [2048], P('head'), may hold values from 0.1 to 1.9
- proj_weight: bfloat16 [2048, 2048], P('head', 'expert'), may hold values from -0.125 to 0.125
- moe_gain: float32 [2048], replicated, may hold values from 0.1 to 1.9
- w_gate: bfloat16 [64, 704, 2048], P(('seq', 'head'), None, 'expert'), may hold values from -0.125 to 0.125
- w_up: bfloat16 [64, 704, 2048], P(('seq', 'head'), None, 'expert'), may hold values from -0.125 to 0.125
- w_down: bfloat16 [64, 704, 2048], P(('seq', 'head'), None, 'expert'), may hold values from -0.21875 to 0.21875
- expert_ids: int32 [8, 4096, 6], P('expert', ('seq', 'head')), may hold values from 0 to 63, all different within a row; in each aligned block of 64 rows (0 to 63, 64 to 127, ..., all dimensions but the last counted through in order) at most 8 rows name the same one
- gate_weights: float32 [8, 4096, 6], P('expert', ('seq', 'head')), may hold values from 0.05 to 0.5
Outputs:
- layer_out: bfloat16 [8, 4096, 2048], P('expert', ('seq', 'head'))
The draws below stay inside these ranges and needn't reach their ends.
Inputs may be any that keep to these rules, and one draw needn't show every extreme that they name: `expert_ids`: each token names 6 different experts. Among the 64 tokens of one device (aligned blocks of 64 positions) no expert is named more than 8 times, a bound that some block reaches.
All inputs are finite; a program needn't handle non-finite values.
Results may differ from the reference program's by a relative error of at most 0.019.
Values may be sent and summed in bfloat16 or wider, within the bound.
A program may use at most 128 MiB of HBM per device.

```python
import math
import jax
import jax.numpy as jnp
import numpy as np
from jax import lax

D = 2048
NH = 16
HD = 128
H = 704
TOP = 6
TOK_DEV = 128
N_SEQS = 8
L = 4096
ROWS = 64
EXPERTS = 64
CAP = 8


def block_scale(key, dims, shards, least, high):
    level, own = 1.0, jax.random.fold_in(key, 6)
    for axis_at, blocks in shards:
        steps = jnp.exp(jax.random.uniform(jax.random.fold_in(own, axis_at), (blocks,), jnp.float32, least / len(shards), high / len(shards)))
        level = level * jnp.repeat(steps, dims[axis_at] // blocks).reshape([-1 if axis == axis_at else 1 for axis in range(len(dims))])
    return level


def deal_out(stream_key, own, number, rows, amount, top, limit, skew):
    sequence = jax.random.permutation(stream_key, amount)
    packed, usual = portions_of(amount, rows * top, limit, skew, True), portions_of(amount, rows * top, limit, skew, False)
    places = jnp.arange(amount)

    def named(lengths, turn):
        used = int((lengths > 0).sum())
        fixed = max(1, used // 4)
        moved = fixed + (places - fixed + turn * (used - fixed)) % max(1, amount - fixed)
        return jnp.zeros((amount,), jnp.int32).at[sequence[jnp.where(places < fixed, places, moved)]].set(jnp.asarray(lengths, jnp.int32))

    lengths = jnp.where(number % 4 == 0, named(packed, number // 4), named(usual, number - number // 4 - 1))
    mixed = jax.random.permutation(jax.random.fold_in(own, 3), amount)
    source_of, receiver = mixed[0:amount // 2 * 2:2], mixed[1:amount // 2 * 2:2]
    margin = jnp.minimum(lengths[source_of] - 1, limit - lengths[receiver]) // 2
    margin = jnp.where((source_of == sequence[0]) | (receiver == sequence[0]) | (lengths[receiver] == 0), 0, jnp.maximum(margin, 0))
    moved = jax.random.randint(jax.random.fold_in(own, 4), (amount // 2,), 0, 1 << 20) % (margin + 1)
    lengths = lengths.at[source_of].add(-moved).at[receiver].add(moved)
    members = jnp.searchsorted(jnp.cumsum(lengths), jnp.arange(rows * top), side="right").astype(jnp.int32)
    table = members.reshape(top, rows).T
    table = table[jax.random.permutation(jax.random.fold_in(own, 1), rows)]
    turn = jax.random.randint(jax.random.fold_in(own, 2), (rows, 1), 0, top)
    return jnp.take_along_axis(table, (jnp.arange(top)[None, :] + turn) % top, axis=1)


def portions_of(count, total, limit, skew, full):
    loads = [(1 << 20) // math.isqrt(rank ** skew) + 1 for rank in range(1, count + 1)]
    largest = limit if full else min(limit, max(-(-total // count), total * loads[0] // sum(loads)))
    least = 1 if total - largest >= count - 1 else 0
    given, spare = [largest] + [least] * (count - 1), total - largest - least * (count - 1)
    while spare > 0:
        candidates = [i for i in range(1, count) if given[i] < largest] or [i for i in range(1, count) if given[i] < limit]
        whole, budget = sum([loads[i] for i in candidates]), spare
        for i in candidates:
            extra = min(limit - given[i], max(1, budget * loads[i] // whole), spare)
            given[i] = given[i] + extra
            spare = spare - extra
    return np.array(given)


def gaussian(stream_key, extent, scale, most, split=(), kind=jnp.bfloat16):
    loudness = block_scale(stream_key, extent, split, -0.22, 0.18) if split else 1.0
    drawn = jax.random.normal(stream_key, extent, jnp.float32) * scale * loudness
    return jnp.minimum(jnp.maximum(drawn, -most), most).astype(kind)


def setup_inputs(seed: int = 0) -> dict:
    streams_of = jax.random.split(jax.random.key(seed), 14)
    query_proj = gaussian(streams_of[0], (N_SEQS, L, NH * HD), 1.0, 6.0, ((0, 8), (1, 32), (2, 2)))
    key_proj = gaussian(streams_of[1], (N_SEQS, L, NH * HD), 1.0, 6.0, ((0, 8), (1, 32), (2, 2)))
    value_proj = gaussian(streams_of[2], (N_SEQS, L, NH * HD), 1.0, 6.0, ((0, 8), (1, 32), (2, 2)))
    init_state = gaussian(streams_of[3], (N_SEQS, NH, HD, HD), (L // 64), 384.0, ((0, 8), (1, 2)), jnp.float32)
    residual = gaussian(streams_of[4], (N_SEQS, L, D), 1.0, 6.0, ((0, 8), (1, 64)))
    out_gain = jnp.clip(1.0 + 0.18 * jax.random.normal(streams_of[5], (NH * HD,), jnp.float32), 0.1, 1.9)
    proj_weight = gaussian(streams_of[6], (NH * HD, D), (NH * HD) ** -0.5, 0.125, ((0, 2), (1, 8)))
    moe_gain = jnp.clip(1.0 + 0.18 * jax.random.normal(streams_of[7], (D,), jnp.float32), 0.1, 1.9)
    w_gate = gaussian(streams_of[8], (EXPERTS, H, D), D ** -0.5, 0.125, ((0, 64), (2, 8)))
    w_up = gaussian(streams_of[9], (EXPERTS, H, D), D ** -0.5, 0.125, ((0, 64), (2, 8)))
    w_down = gaussian(streams_of[10], (EXPERTS, H, D), H ** -0.5, 0.21875, ((0, 64), (2, 8)))
    expert_ids_keys = jax.random.split(jax.random.fold_in(streams_of[11], 1), N_SEQS * L // ROWS)
    expert_ids_turns = jax.random.permutation(jax.random.fold_in(streams_of[11], 3), N_SEQS * L // ROWS)
    expert_ids = jax.vmap(lambda own, number: deal_out(jax.random.fold_in(streams_of[11], 2), own, number, ROWS, EXPERTS, TOP, CAP, 2))(expert_ids_keys, expert_ids_turns).reshape((N_SEQS, L, TOP))
    gate_weights = jnp.clip(jnp.exp(math.log(0.5) - 2.3025851 * jax.random.uniform(streams_of[12], (N_SEQS, L, TOP), jnp.float32) ** block_scale(streams_of[12], (N_SEQS, L, TOP), ((0, 8), (1, 64)), -0.2, 0.2)), 0.05, 0.5)
    return {"query_proj": query_proj, "key_proj": key_proj, "value_proj": value_proj, "init_state": init_state, "residual": residual, "out_gain": out_gain, "proj_weight": proj_weight, "moe_gain": moe_gain, "w_gate": w_gate, "w_up": w_up, "w_down": w_down, "expert_ids": expert_ids, "gate_weights": gate_weights}


HIGHEST = lax.Precision.HIGHEST

def attend_sequence(quad):
    query_seq, key_seq, value_seq, start_state = quad
    length = query_seq.shape[0]
    pieces = length // TOK_DEV

    def to_blocks(matrix):
        return matrix.astype(jnp.float32).reshape(pieces, TOK_DEV, NH, HD).transpose(0, 2, 1, 3)
    causal = jnp.tril(jnp.ones((TOK_DEV, TOK_DEV), jnp.float32))

    def advance(state, inputs):
        query_blk, key_blk, value_blk = inputs
        scores = jnp.einsum('htd,hsd->hts', query_blk, key_blk, precision=HIGHEST) * causal
        within = jnp.einsum('hts,hsd->htd', scores, value_blk, precision=HIGHEST)
        carried = jnp.einsum('htd,hde->hte', query_blk, state, precision=HIGHEST)
        state = state + jnp.einsum('hsd,hse->hde', key_blk, value_blk, precision=HIGHEST)
        return (state, within + carried)
    initial = start_state.astype(jnp.float32)
    final_state, result = lax.scan(advance, initial, (to_blocks(query_seq), to_blocks(key_seq), to_blocks(value_seq)))
    return result.transpose(0, 2, 1, 3).reshape(length, NH, HD)

def reference(query_proj, key_proj, value_proj, init_state, residual, out_gain, proj_weight, moe_gain, w_gate, w_up, w_down, expert_ids, gate_weights):
    attended = lax.map(attend_sequence, (query_proj, key_proj, value_proj, init_state))
    inv_norm = lax.rsqrt(lax.optimization_barrier(jnp.mean(attended * attended, axis=-1, keepdims=True)) + 1e-05)
    normed = ((attended * inv_norm).reshape(N_SEQS * L, NH * HD) * out_gain).astype(jnp.bfloat16)
    projected = jnp.dot(normed, proj_weight, preferred_element_type=jnp.float32)
    stream = (residual.reshape(N_SEQS * L, D).astype(jnp.float32) + projected).astype(jnp.bfloat16)
    stream_f = lax.optimization_barrier(stream).astype(jnp.float32)
    moe_in = (stream_f * lax.rsqrt(lax.optimization_barrier(jnp.mean(stream_f * stream_f, axis=-1, keepdims=True)) + 1e-06) * moe_gain).astype(jnp.bfloat16)
    chosen_ids = expert_ids.reshape(N_SEQS * L, TOP)
    chosen_weights = gate_weights.reshape(N_SEQS * L, TOP)
    bound = N_SEQS * L // ROWS * CAP

    def one_expert(accum, inputs):
        index, gate_mat, up_mat, down_mat = inputs
        matches = chosen_ids == index
        selected = jnp.any(matches, axis=1)
        weight = lax.optimization_barrier(jnp.sum(jnp.where(matches, chosen_weights, 0.0), axis=1))
        number = jnp.sum(selected.astype(jnp.int32))
        positions = jnp.nonzero(selected, size=bound, fill_value=0)[0].astype(jnp.int32)
        picked = moe_in[positions]
        gate_act = lax.dot_general(picked, gate_mat, (((1,), (1,)), ((), ())), preferred_element_type=jnp.float32)
        up_act = lax.dot_general(picked, up_mat, (((1,), (1,)), ((), ())), preferred_element_type=jnp.float32)
        hidden = (jax.nn.silu(gate_act) * up_act).astype(jnp.bfloat16)
        expert_out = jnp.dot(hidden, down_mat, preferred_element_type=jnp.float32).astype(jnp.bfloat16)
        valid = jnp.arange(bound, dtype=jnp.int32) < number
        contrib = jnp.where(valid[:, None], weight[positions][:, None] * expert_out.astype(jnp.float32), 0.0)
        return (accum.at[positions].add(contrib), None)
    zeros_acc = jnp.zeros((N_SEQS * L, D), jnp.float32)
    summed, unused = lax.scan(one_expert, zeros_acc, (jnp.arange(EXPERTS, dtype=jnp.int32), w_gate, w_up, w_down))
    return (stream_f + summed).astype(jnp.bfloat16).reshape(N_SEQS, L, D)
```

```python
import functools

import jax
import jax.numpy as jnp
from jax import lax
from jax.experimental import pallas as pl
from jax.experimental.pallas import tpu as pltpu
from jax.sharding import PartitionSpec as P

D = 2048
HALF = 1024
HD = 128
TOP = 6
CAP = 8
BLK = 2 * CAP
MESH = pl.DeviceIdType.MESH
BF16 = jnp.bfloat16
F32 = jnp.float32
VMEM_LIMIT = 56 * 2**20


def grid_of(seq):
    nx = 4 if seq == 32 else 2
    return nx, seq // nx


def dot(a, b, dims=((1,), (0,))):
    return lax.dot_general(a, b, (dims, ((), ())), preferred_element_type=F32)


def rows(index, size):
    return pl.ds(pl.multiple_of(index * size, size), size)


def remote(src, dst, send, recv, target):
    return pltpu.make_async_remote_copy(
        src_ref=src, dst_ref=dst, send_sem=send, recv_sem=recv, device_id=target, device_id_type=MESH
    )


def attend_kernel(
    nx, ny, q_ref, k_ref, v_ref, init_ref, gain_ref, mixed_ref,
    loc, xin, tot, yin, pre, pin, att, x_send, x_recv, y_send, y_recv, p_send, p_recv,
):
    s, h, z = lax.axis_index("seq"), lax.axis_index("head"), lax.axis_index("expert")
    y, x = s // nx, lax.rem(s, nx)
    heads = q_ref.shape[1] // HD
    part = heads // nx

    def at_x(d):
        return (y * nx + lax.rem(x + d, nx), h, z)

    def at_y(d):
        return (lax.rem(y + d, ny) * nx + x, h, z)

    barrier = pltpu.get_barrier_semaphore()
    for d in range(1, nx):
        pl.semaphore_signal(barrier, inc=1, device_id=at_x(d), device_id_type=MESH)
    for d in range(1, ny):
        pl.semaphore_signal(barrier, inc=1, device_id=at_y(d), device_id_type=MESH)
    for i in range(heads):
        cols = slice(i * HD, (i + 1) * HD)
        loc[i // part, i % part] = dot(k_ref[:, cols], v_ref[:, cols], ((0,), (0,))).astype(BF16)
    pl.semaphore_wait(barrier, nx - 1 + ny - 1)

    first = [
        remote(loc.at[lax.rem(x + d, nx)], xin.at[d], x_send.at[d], x_recv.at[d], at_x(d))
        for d in range(1, nx)
    ]
    for copy in first:
        copy.start()
    xin[0] = loc[x]
    for copy in first:
        copy.wait_recv()
    tot[...] = sum(xin[d].astype(F32) for d in range(nx)).astype(BF16)
    second = [remote(tot, yin.at[d], y_send.at[d], y_recv.at[d], at_y(d)) for d in range(1, ny)]
    for copy in second:
        copy.start()

    tokens = q_ref.shape[0]
    causal = lax.broadcasted_iota(jnp.int32, (tokens, tokens), 0) >= lax.broadcasted_iota(
        jnp.int32, (tokens, tokens), 1
    )
    for i in range(heads):
        cols = slice(i * HD, (i + 1) * HD)
        scores = dot(q_ref[:, cols], k_ref[:, cols], ((1,), (1,)))
        scores = jnp.where(causal, scores, 0.0).astype(BF16)
        att[:, cols] = dot(scores, v_ref[:, cols])

    before = jnp.zeros(tot.shape, F32)
    for d in range(1, ny):
        second[d - 1].wait_recv()
        before = before + yin[d].astype(F32) * (d <= y).astype(F32)
    third = []
    for e in range(nx):
        target = lax.rem(x + e, nx)
        state = before
        for d in range(nx):
            source = lax.rem(x + nx - d, nx)
            state = state + xin[d].astype(F32) * (source < target).astype(F32)
        pre[e] = state.astype(BF16)
        if e:
            copy = remote(pre.at[e], pin.at[e], p_send.at[e], p_recv.at[e], at_x(e))
            copy.start()
            third.append(copy)
    pin[0] = pre[0]
    for e in range(nx):
        if e:
            third[e - 1].wait_recv()
        for j in range(part):
            head = lax.rem(x + nx - e, nx) * part + j
            cols = rows(head, HD)
            state = (init_ref[head] + pin[e, j].astype(F32)).astype(BF16)
            out = att[:, cols] + dot(q_ref[:, cols], state)
            inv = lax.rsqrt(jnp.mean(out * out, axis=1, keepdims=True) + 1e-05)
            mixed_ref[:, cols] = (out * inv * gain_ref[:, cols]).astype(BF16)
    for copy in first + second + third:
        copy.wait_send()


def place(ids_ref, gates_ref, placing, weighing):
    tokens = ids_ref.shape[0]
    slots = placing.shape[1]
    experts = slots // BLK
    expert = lax.broadcasted_iota(jnp.int32, (tokens, experts), 1)
    chosen = jnp.zeros((tokens, experts), F32)
    gates = jnp.zeros((tokens, experts), F32)
    for k in range(TOP):
        match = ids_ref[:, k : k + 1] == expert
        chosen = chosen + jnp.where(match, 1.0, 0.0)
        gates = gates + jnp.where(match, gates_ref[:, k : k + 1], 0.0)
    earlier = lax.broadcasted_iota(jnp.int32, (tokens, tokens), 1) < lax.broadcasted_iota(
        jnp.int32, (tokens, tokens), 0
    )
    earlier = jnp.where(earlier, 1.0, 0.0).astype(BF16)
    order = dot(earlier, chosen.astype(BF16))
    turn = (chosen * (order + 1.0)).astype(BF16)
    spread = lax.broadcasted_iota(jnp.int32, (experts, slots), 1) // BLK == lax.broadcasted_iota(
        jnp.int32, (experts, slots), 0
    )
    spread = jnp.where(spread, 1.0, 0.0).astype(BF16)
    turn = dot(turn, spread)
    gates = dot(gates.astype(BF16), spread)
    slot = lax.broadcasted_iota(jnp.int32, (tokens, slots), 1)
    place_in = lax.rem(slot, BLK)
    for half in range(2):
        wanted = (place_in - (half * CAP - 1)).astype(F32)
        hit = (turn == wanted) & (place_in // CAP == half)
        span = slice(half * tokens, (half + 1) * tokens)
        placing[span, :] = jnp.where(hit, 1.0, 0.0).astype(BF16)
        weighing[span, :] = jnp.where(hit, gates, 0.0).astype(BF16)


def dispatch_kernel(
    mixed_ref, wo_ref, res_ref, gain_ref, ids_ref, gates_ref, stream_ref, weigh_ref, incoming_ref,
    proj, snd, rcv, placing, feats, outgoing, h_sem, own_sem, send, recv,
):
    s, h, z = lax.axis_index("seq"), lax.axis_index("head"), lax.axis_index("expert")
    count = lax.axis_size("seq") * lax.axis_size("head")
    me = s * 2 + h
    tokens = res_ref.shape[0]

    def device(index):
        return (index // 2, lax.rem(index, 2), z)

    barrier = pltpu.get_barrier_semaphore()

    def greet(off, carry):
        pl.semaphore_signal(
            barrier, inc=1, device_id=device(lax.rem(me + off, count)), device_id_type=MESH
        )
        return carry

    lax.fori_loop(1, count, greet, 0)
    width = 512
    for c in range(D // width):
        cols = slice(c * width, (c + 1) * width)
        proj[:, cols] = dot(mixed_ref[...], wo_ref[:, cols])
    snd[...] = proj[rows(1 - h, tokens), :].astype(BF16)
    pl.semaphore_wait(barrier, count - 1)
    half = remote(snd, rcv, h_sem.at[0], h_sem.at[1], (s, 1 - h, z))
    half.start()
    place(ids_ref, gates_ref, placing, weigh_ref)
    half.wait_recv()
    stream = (
        res_ref[...].astype(F32) + (proj[rows(h, tokens), :] + rcv[...].astype(F32))
    ).astype(BF16)
    stream_ref[...] = stream
    stream_f = stream.astype(F32)
    inv = lax.rsqrt(jnp.mean(stream_f * stream_f, axis=1, keepdims=True) + 1e-06)
    moe_in = (stream_f * inv * gain_ref[...]).astype(BF16)
    feats[:tokens, :] = moe_in[:, :HALF]
    feats[tokens:, :] = moe_in[:, HALF:]
    tile = 256
    for c in range(outgoing.shape[0] // tile):
        span = slice(c * tile, (c + 1) * tile)
        outgoing[span, :] = dot(placing[:, span], feats[...], ((0,), (0,))).astype(BF16)

    def block(off):
        target = lax.rem(me + off, count)
        return remote(
            outgoing.at[rows(target, BLK), :], incoming_ref.at[rows(off, BLK), :],
            send.at[off], recv.at[off], device(target),
        )

    def begin(off, carry):
        block(off).start()
        return carry

    def finish(off, carry):
        block(off).wait()
        return carry

    lax.fori_loop(1, count, begin, 0)
    own = pltpu.make_async_copy(
        outgoing.at[rows(me, BLK), :], incoming_ref.at[pl.ds(0, BLK), :], own_sem
    )
    own.start()
    own.wait()
    half.wait_send()
    lax.fori_loop(1, count, finish, 0)


def expert_kernel(
    x_ref, w_ref, stream_ref, weigh_ref, out_ref, results, returned, own_sem, send, recv
):
    s, h, z = lax.axis_index("seq"), lax.axis_index("head"), lax.axis_index("expert")
    count = lax.axis_size("seq") * lax.axis_size("head")
    me = s * 2 + h
    tokens = stream_ref.shape[0]
    hidden_width = w_ref.shape[0] // 3

    def device(index):
        return (index // 2, lax.rem(index, 2), z)

    barrier = pltpu.get_barrier_semaphore()

    def greet(off, carry):
        pl.semaphore_signal(
            barrier, inc=1, device_id=device(lax.rem(me + off, count)), device_id_type=MESH
        )
        return carry

    lax.fori_loop(1, count, greet, 0)

    def block(off):
        return remote(
            results.at[rows(off, BLK), :], returned.at[rows(me, BLK), :],
            send.at[off], recv.at[off], device(lax.rem(me + count - off, count)),
        )

    def begin(off, carry):
        block(off).start()
        return carry

    group = count // 2
    for c in range(2):
        span = slice(c * group * BLK, (c + 1) * group * BLK)
        x = x_ref[span, :].astype(F32).reshape(group, BLK, HALF)
        low = x[:, :CAP].reshape(group * CAP, HALF).astype(BF16)
        high = x[:, CAP:].reshape(group * CAP, HALF).astype(BF16)
        acts = []
        for i in range(2):
            span_w = slice(i * hidden_width, (i + 1) * hidden_width)
            acts.append(
                dot(low, w_ref[span_w, :HALF], ((1,), (1,)))
                + dot(high, w_ref[span_w, HALF:], ((1,), (1,)))
            )
        gate, up = acts
        hidden = (gate / (1.0 + jnp.exp(-gate)) * up).astype(BF16)
        outs = [
            dot(hidden, w_ref[2 * hidden_width :, i * HALF : (i + 1) * HALF]).reshape(group, CAP, HALF)
            for i in range(2)
        ]
        results[span, :] = jnp.concatenate(outs, axis=1).reshape(group * BLK, HALF).astype(BF16)
        if c == 0:
            pl.semaphore_wait(barrier, count - 1)
        lax.fori_loop(max(1, c * group), (c + 1) * group, begin, 0)
    own = pltpu.make_async_copy(
        results.at[pl.ds(0, BLK), :], returned.at[rows(me, BLK), :], own_sem
    )
    own.start()
    own.wait()

    def finish(off, carry):
        source = lax.rem(me + off, count)
        block(off).wait_send()
        remote(
            results.at[rows(off, BLK), :], returned.at[rows(source, BLK), :],
            send.at[off], recv.at[off], device(source),
        ).wait_recv()
        return carry

    lax.fori_loop(1, count, finish, 0)
    combined = dot(weigh_ref[...], returned[...])
    for half in range(2):
        cols = slice(half * HALF, (half + 1) * HALF)
        span = slice(half * tokens, (half + 1) * tokens)
        out_ref[:, cols] = (stream_ref[:, cols].astype(F32) + combined[span, :]).astype(BF16)


def in_vmem(n):
    return [pl.BlockSpec(memory_space=pltpu.VMEM)] * n


def shards(
    nx, ny,
    query_proj, key_proj, value_proj, init_state, residual, out_gain, proj_weight, moe_gain,
    w_gate, w_up, w_down, expert_ids, gate_weights,
):
    tok, width = query_proj.shape[1:]
    heads = width // HD
    part = heads // nx
    token_rows = residual.shape[1]
    count = nx * ny * 2
    slots = count * BLK

    wo_full = lax.all_gather(proj_weight, "expert", axis=1, tiled=True)
    stacked = jnp.concatenate([w_gate[0], w_up[0], w_down[0]], axis=0)
    w_full = lax.all_gather(stacked, "expert", axis=1, tiled=True)

    state = (part, HD, HD)
    mixed = pl.pallas_call(
        functools.partial(attend_kernel, nx, ny),
        out_shape=jax.ShapeDtypeStruct((tok, width), BF16),
        in_specs=in_vmem(5),
        out_specs=pl.BlockSpec(memory_space=pltpu.VMEM),
        scratch_shapes=[
            pltpu.VMEM((nx, *state), BF16),
            pltpu.VMEM((nx, *state), BF16),
            pltpu.VMEM(state, BF16),
            pltpu.VMEM((ny, *state), BF16),
            pltpu.VMEM((nx, *state), BF16),
            pltpu.VMEM((nx, *state), BF16),
            pltpu.VMEM((tok, width), F32),
            pltpu.SemaphoreType.DMA((nx,)),
            pltpu.SemaphoreType.DMA((nx,)),
            pltpu.SemaphoreType.DMA((ny,)),
            pltpu.SemaphoreType.DMA((ny,)),
            pltpu.SemaphoreType.DMA((nx,)),
            pltpu.SemaphoreType.DMA((nx,)),
        ],
        compiler_params=pltpu.CompilerParams(
            collective_id=0, has_side_effects=True, vmem_limit_bytes=VMEM_LIMIT
        ),
        cost_estimate=pl.CostEstimate(flops=10**9, bytes_accessed=10**8, transcendentals=0),
        name="attend",
    )(query_proj[0], key_proj[0], value_proj[0], init_state[0], out_gain[None, :])

    stream, weighing, incoming = pl.pallas_call(
        dispatch_kernel,
        out_shape=[
            jax.ShapeDtypeStruct((token_rows, D), BF16),
            jax.ShapeDtypeStruct((2 * token_rows, slots), BF16),
            jax.ShapeDtypeStruct((slots, HALF), BF16),
        ],
        in_specs=in_vmem(6),
        out_specs=[*in_vmem(2), pl.BlockSpec(memory_space=pl.ANY)],
        scratch_shapes=[
            pltpu.VMEM((tok, D), F32),
            pltpu.VMEM((token_rows, D), BF16),
            pltpu.VMEM((token_rows, D), BF16),
            pltpu.VMEM((2 * token_rows, slots), BF16),
            pltpu.VMEM((2 * token_rows, HALF), BF16),
            pltpu.VMEM((slots, HALF), BF16),
            pltpu.SemaphoreType.DMA((2,)),
            pltpu.SemaphoreType.DMA,
            pltpu.SemaphoreType.DMA((count,)),
            pltpu.SemaphoreType.DMA((count,)),
        ],
        compiler_params=pltpu.CompilerParams(
            collective_id=1, has_side_effects=True, vmem_limit_bytes=VMEM_LIMIT
        ),
        cost_estimate=pl.CostEstimate(flops=10**9, bytes_accessed=2 * 10**8, transcendentals=0),
        name="dispatch",
    )(mixed, wo_full, residual[0], moe_gain[None, :], expert_ids[0], gate_weights[0])

    out = pl.pallas_call(
        expert_kernel,
        out_shape=jax.ShapeDtypeStruct((token_rows, D), BF16),
        in_specs=in_vmem(4),
        out_specs=pl.BlockSpec(memory_space=pltpu.VMEM),
        scratch_shapes=[
            pltpu.VMEM((slots, HALF), BF16),
            pltpu.VMEM((slots, HALF), BF16),
            pltpu.SemaphoreType.DMA,
            pltpu.SemaphoreType.DMA((count,)),
            pltpu.SemaphoreType.DMA((count,)),
        ],
        compiler_params=pltpu.CompilerParams(
            collective_id=2, has_side_effects=True, vmem_limit_bytes=VMEM_LIMIT
        ),
        cost_estimate=pl.CostEstimate(flops=5 * 10**9, bytes_accessed=2 * 10**8, transcendentals=0),
        name="experts",
    )(incoming, w_full, stream, weighing)
    return out[None]


def solution(mesh):
    placed = (
        P("expert", "seq", "head"),
        P("expert", "seq", "head"),
        P("expert", "seq", "head"),
        P("expert", "head", None, None),
        P("expert", ("seq", "head"), None),
        P("head"),
        P("head", "expert"),
        P(),
        P(("seq", "head"), None, "expert"),
        P(("seq", "head"), None, "expert"),
        P(("seq", "head"), None, "expert"),
        P("expert", ("seq", "head"), None),
        P("expert", ("seq", "head"), None),
    )
    nx, ny = grid_of(mesh.shape["seq"])
    return jax.shard_map(
        functools.partial(shards, nx, ny),
        mesh=mesh,
        in_specs=placed,
        out_specs=P("expert", ("seq", "head"), None),
        check_vma=False,
    )
```

```python
import functools

import jax
import jax.numpy as jnp
from jax import lax
from jax.experimental import pallas as pl
from jax.experimental.pallas import tpu as pltpu
from jax.sharding import PartitionSpec as P

D = 2048
HALF = 1024
HD = 128
TOP = 6
CAP = 8
BLK = 2 * CAP
MESH = pl.DeviceIdType.MESH
BF16 = jnp.bfloat16
F32 = jnp.float32
VMEM_LIMIT = 56 * 2**20


def grid_of(seq):
    nx = 4 if seq == 32 else 2
    return nx, seq // nx


def dot(a, b, dims=((1,), (0,))):
    return lax.dot_general(a, b, (dims, ((), ())), preferred_element_type=F32)


def rows(index, size):
    return pl.ds(pl.multiple_of(index * size, size), size)


def remote(src, dst, send, recv, target):
    return pltpu.make_async_remote_copy(
        src_ref=src, dst_ref=dst, send_sem=send, recv_sem=recv, device_id=target, device_id_type=MESH
    )


def place(ids_ref, gates_ref, placing, weighing):
    tokens = ids_ref.shape[0]
    slots = placing.shape[1]
    experts = slots // BLK
    expert = lax.broadcasted_iota(jnp.int32, (tokens, experts), 1)
    chosen = jnp.zeros((tokens, experts), F32)
    gates = jnp.zeros((tokens, experts), F32)
    for k in range(TOP):
        match = ids_ref[:, k : k + 1] == expert
        chosen = chosen + jnp.where(match, 1.0, 0.0)
        gates = gates + jnp.where(match, gates_ref[:, k : k + 1], 0.0)
    earlier = lax.broadcasted_iota(jnp.int32, (tokens, tokens), 1) < lax.broadcasted_iota(
        jnp.int32, (tokens, tokens), 0
    )
    earlier = jnp.where(earlier, 1.0, 0.0).astype(BF16)
    order = dot(earlier, chosen.astype(BF16))
    turn = (chosen * (order + 1.0)).astype(BF16)
    spread = lax.broadcasted_iota(jnp.int32, (experts, slots), 1) // BLK == lax.broadcasted_iota(
        jnp.int32, (experts, slots), 0
    )
    spread = jnp.where(spread, 1.0, 0.0).astype(BF16)
    turn = dot(turn, spread)
    gates = dot(gates.astype(BF16), spread)
    slot = lax.broadcasted_iota(jnp.int32, (tokens, slots), 1)
    place_in = lax.rem(slot, BLK)
    for half in range(2):
        wanted = (place_in - (half * CAP - 1)).astype(F32)
        hit = (turn == wanted) & (place_in // CAP == half)
        span = slice(half * tokens, (half + 1) * tokens)
        placing[span, :] = jnp.where(hit, 1.0, 0.0).astype(BF16)
        weighing[span, :] = jnp.where(hit, gates, 0.0).astype(BF16)


def front_kernel(
    nx, ny, nz, q_ref, k_ref, v_ref, init_ref, out_gain_ref, wo_ref, res_ref, gain_ref, ids_ref, gates_ref,
    stream_ref, weigh_ref, incoming_ref,
    loc, xin, tot, yin, pre, pin, att, mixed, wo, proj, snd, rcv, placing, feats, outgoing,
    x_send, x_recv, y_send, y_recv, p_send, p_recv, wz_send, wz_recv, wy_send, wy_recv,
    right_send, right_recv, left_send, left_recv, pass_send, pass_recv, h_sem, own_sem, send, recv,
):
    s, h, z = lax.axis_index("seq"), lax.axis_index("head"), lax.axis_index("expert")
    y, x = s // nx, lax.rem(s, nx)
    count = nx * ny * 2
    me = s * 2 + h
    heads = q_ref.shape[1] // HD
    part = heads // nx
    tokens = res_ref.shape[0]
    depth = wo_ref.shape[0] // (nx * ny)
    width = wo_ref.shape[1]

    def device(index):
        return (index // 2, lax.rem(index, 2), z)

    def at_x(d):
        return (y * nx + lax.rem(x + d, nx), h, z)

    def at_y(d):
        return (lax.rem(y + d, ny) * nx + x, h, z)

    def at_z(d):
        return (s, h, lax.rem(z + d, nz))

    barrier = pltpu.get_barrier_semaphore()
    for d in range(1, nz):
        pl.semaphore_signal(barrier, inc=1, device_id=at_z(d), device_id_type=MESH)

    def greet(off, carry):
        pl.semaphore_signal(
            barrier, inc=1, device_id=device(lax.rem(me + off, count)), device_id_type=MESH
        )
        return carry

    with jax.named_scope("greet"):
        lax.fori_loop(1, count, greet, 0)
    with jax.named_scope("states"):
        for i in range(heads):
            cols = slice(i * HD, (i + 1) * HD)
            loc[i // part, i % part] = dot(k_ref[:, cols], v_ref[:, cols], ((0,), (0,))).astype(BF16)
    with jax.named_scope("barrier"):
        pl.semaphore_wait(barrier, count - 1 + nz - 1)

    first = [
        remote(loc.at[lax.rem(x + d, nx)], xin.at[d], x_send.at[d], x_recv.at[d], at_x(d))
        for d in range(1, nx)
    ]
    for copy in first:
        copy.start()

    def strip(dx, dy):
        return pl.ds(
            pl.multiple_of((lax.rem(x + dx, nx) * ny + lax.rem(y + dy, ny)) * depth, depth), depth
        )

    mine = strip(0, 0)

    def fetch(d, owner):
        return remote(
            wo_ref.at[mine, :], wo.at[owner, mine, :], wz_send.at[d], wz_recv.at[d], at_z(d)
        )

    for d in range(1, nz):
        fetch(d, z).start()

    def along_y(b, step):
        block = wo.at[:, strip(0, ny - b), :]
        arrives = (b + step) % ny
        return remote(block, block, wy_send.at[arrives], wy_recv.at[arrives], at_y(step))

    def landed_y(b, step):
        block = wo.at[:, strip(0, ny - b), :]
        return remote(block, block, wy_send.at[b], wy_recv.at[b], at_y(step))

    def along_x(b, dx, sends, recvs, step):
        block = wo.at[:, strip(dx, ny - b), :]
        return remote(block, block, sends.at[b], recvs.at[b], at_x(step))

    reach = ny // 2
    to_right = [0, *range(reach + 1, ny)]

    def spread(b):
        along_x(b, 0, right_send, right_recv, 1).start()
        along_x(b, 0, left_send, left_recv, nx - 1).start()

    def relay_y(b):
        if b <= reach:
            landed_y(b, 1).wait_recv()
            if b < reach:
                along_y(b, 1).start()
        else:
            landed_y(b, ny - 1).wait_recv()
            if b > reach + 1:
                along_y(b, ny - 1).start()
        spread(b)

    def relay_x(b):
        if b in to_right:
            along_x(b, nx - 1, right_send, right_recv, 1).wait_recv()
            along_x(b, nx - 1, pass_send, pass_recv, 1).start()
        else:
            along_x(b, 1, left_send, left_recv, nx - 1).wait_recv()
            along_x(b, 1, pass_send, pass_recv, nx - 1).start()

    with jax.named_scope("states_x"):
        xin[0] = loc[x]
        for copy in first:
            copy.wait_recv()
    tot[...] = sum(xin[d].astype(F32) for d in range(nx)).astype(BF16)
    second = [remote(tot, yin.at[d], y_send.at[d], y_recv.at[d], at_y(d)) for d in range(1, ny)]
    for copy in second:
        copy.start()

    with jax.named_scope("fetched"):
        wo[z, mine, :] = wo_ref[mine, :]
        for d in range(1, nz):
            fetch(d, lax.rem(z + nz - d, nz)).wait_recv()
    along_y(0, 1).start()
    along_y(0, ny - 1).start()
    spread(0)

    with jax.named_scope("inner"):
        positions = q_ref.shape[0]
        causal = lax.broadcasted_iota(jnp.int32, (positions, positions), 0) >= lax.broadcasted_iota(
            jnp.int32, (positions, positions), 1
        )
        for i in range(heads):
            cols = slice(i * HD, (i + 1) * HD)
            scores = dot(q_ref[:, cols], k_ref[:, cols], ((1,), (1,)))
            scores = jnp.where(causal, scores, 0.0).astype(BF16)
            att[:, cols] = dot(scores, v_ref[:, cols])
    with jax.named_scope("placing"):
        place(ids_ref, gates_ref, placing, weigh_ref)
    with jax.named_scope("relay_1"):
        relay_y(1)
        relay_y(ny - 1)
        relay_x(0)

    before = jnp.zeros(tot.shape, F32)
    with jax.named_scope("states_y"):
        for d in range(1, ny):
            second[d - 1].wait_recv()
            before = before + yin[d].astype(F32) * (d <= y).astype(F32)
    third = []
    for e in range(nx):
        target = lax.rem(x + e, nx)
        state = before
        for d in range(nx):
            source = lax.rem(x + nx - d, nx)
            state = state + xin[d].astype(F32) * (source < target).astype(F32)
        pre[e] = state.astype(BF16)
        if e:
            copy = remote(pre.at[e], pin.at[e], p_send.at[e], p_recv.at[e], at_x(e))
            copy.start()
            third.append(copy)
    pin[0] = pre[0]
    with jax.named_scope("relay_2"):
        for step in range(2, reach):
            relay_y(step)
            relay_y(ny - step)
            relay_x(step - 1)
            relay_x(ny - step + 1)
        relay_y(reach)
        relay_x(reach - 1)
        relay_x(reach + 1)
    with jax.named_scope("mix"):
        for e in range(nx):
            if e:
                third[e - 1].wait_recv()
            for j in range(part):
                head = lax.rem(x + nx - e, nx) * part + j
                cols = rows(head, HD)
                state = (init_ref[head] + pin[e, j].astype(F32)).astype(BF16)
                out = att[:, cols] + dot(q_ref[:, cols], state)
                inv = lax.rsqrt(jnp.mean(out * out, axis=1, keepdims=True) + 1e-05)
                mixed[:, cols] = (out * inv * out_gain_ref[:, cols]).astype(BF16)
    with jax.named_scope("relay_3"):
        relay_x(reach)
        for b in range(ny):
            if b in to_right:
                along_x(b, 1, left_send, left_recv, nx - 1).wait_recv()
                along_x(b, 2, pass_send, pass_recv, 1).wait_recv()
            else:
                along_x(b, nx - 1, right_send, right_recv, 1).wait_recv()
                along_x(b, 2, pass_send, pass_recv, nx - 1).wait_recv()

    with jax.named_scope("project"):
        for c in range(nz):
            proj[:, c * width : (c + 1) * width] = dot(mixed[...], wo[c])
    snd[...] = proj[rows(1 - h, tokens), :].astype(BF16)
    half = remote(snd, rcv, h_sem.at[0], h_sem.at[1], (s, 1 - h, z))
    half.start()
    for copy in first + second + third:
        copy.wait_send()
    for d in range(1, nz):
        fetch(d, z).wait_send()
    for b in range(ny):
        along_x(b, 0, right_send, right_recv, 1).wait_send()
        along_x(b, 0, left_send, left_recv, nx - 1).wait_send()
        if b in to_right:
            along_x(b, nx - 1, pass_send, pass_recv, 1).wait_send()
        else:
            along_x(b, 1, pass_send, pass_recv, nx - 1).wait_send()
        if b and b <= reach:
            along_y(b - 1, 1).wait_send()
        elif b:
            along_y((b + 1) % ny, ny - 1).wait_send()
    with jax.named_scope("other_half"):
        half.wait_recv()
    stream = (
        res_ref[...].astype(F32) + (proj[rows(h, tokens), :] + rcv[...].astype(F32))
    ).astype(BF16)
    stream_ref[...] = stream
    stream_f = stream.astype(F32)
    inv = lax.rsqrt(jnp.mean(stream_f * stream_f, axis=1, keepdims=True) + 1e-06)
    moe_in = (stream_f * inv * gain_ref[...]).astype(BF16)
    feats[:tokens, :] = moe_in[:, :HALF]
    feats[tokens:, :] = moe_in[:, HALF:]
    with jax.named_scope("outgoing"):
        tile = 256
        for c in range(outgoing.shape[0] // tile):
            span = slice(c * tile, (c + 1) * tile)
            outgoing[span, :] = dot(placing[:, span], feats[...], ((0,), (0,))).astype(BF16)

    def block(off):
        target = lax.rem(me + off, count)
        return remote(
            outgoing.at[rows(target, BLK), :], incoming_ref.at[rows(off, BLK), :],
            send.at[off], recv.at[off], device(target),
        )

    def begin(off, carry):
        block(off).start()
        return carry

    def finish(off, carry):
        block(off).wait()
        return carry

    with jax.named_scope("begin"):
        lax.fori_loop(1, count, begin, 0)
    own = pltpu.make_async_copy(
        outgoing.at[rows(me, BLK), :], incoming_ref.at[pl.ds(0, BLK), :], own_sem
    )
    own.start()
    own.wait()
    half.wait_send()
    with jax.named_scope("arrivals"):
        lax.fori_loop(1, count, finish, 0)


def expert_kernel(
    x_ref, w_ref, stream_ref, weigh_ref, out_ref, results, returned, own_sem, send, recv
):
    s, h, z = lax.axis_index("seq"), lax.axis_index("head"), lax.axis_index("expert")
    count = lax.axis_size("seq") * lax.axis_size("head")
    me = s * 2 + h
    tokens = stream_ref.shape[0]
    hidden_width = w_ref.shape[0] // 3

    def device(index):
        return (index // 2, lax.rem(index, 2), z)

    barrier = pltpu.get_barrier_semaphore()

    def greet(off, carry):
        pl.semaphore_signal(
            barrier, inc=1, device_id=device(lax.rem(me + off, count)), device_id_type=MESH
        )
        return carry

    with jax.named_scope("greet"):
        lax.fori_loop(1, count, greet, 0)

    def block(off):
        return remote(
            results.at[rows(off, BLK), :], returned.at[rows(me, BLK), :],
            send.at[off], recv.at[off], device(lax.rem(me + count - off, count)),
        )

    def begin(off, carry):
        block(off).start()
        return carry

    with jax.named_scope("experts"):
        group = count // 2
        for c in range(2):
            span = slice(c * group * BLK, (c + 1) * group * BLK)
            x = x_ref[span, :].astype(F32).reshape(group, BLK, HALF)
            low = x[:, :CAP].reshape(group * CAP, HALF).astype(BF16)
            high = x[:, CAP:].reshape(group * CAP, HALF).astype(BF16)
            acts = []
            for i in range(2):
                span_w = slice(i * hidden_width, (i + 1) * hidden_width)
                acts.append(
                    dot(low, w_ref[span_w, :HALF], ((1,), (1,)))
                    + dot(high, w_ref[span_w, HALF:], ((1,), (1,)))
                )
            gate, up = acts
            hidden = (gate / (1.0 + jnp.exp(-gate)) * up).astype(BF16)
            outs = [
                dot(hidden, w_ref[2 * hidden_width :, i * HALF : (i + 1) * HALF]).reshape(group, CAP, HALF)
                for i in range(2)
            ]
            results[span, :] = jnp.concatenate(outs, axis=1).reshape(group * BLK, HALF).astype(BF16)
            if c == 0:
                pl.semaphore_wait(barrier, count - 1)
            lax.fori_loop(max(1, c * group), (c + 1) * group, begin, 0)
    own = pltpu.make_async_copy(
        results.at[pl.ds(0, BLK), :], returned.at[rows(me, BLK), :], own_sem
    )
    own.start()
    own.wait()

    def finish(off, carry):
        source = lax.rem(me + off, count)
        block(off).wait_send()
        remote(
            results.at[rows(off, BLK), :], returned.at[rows(source, BLK), :],
            send.at[off], recv.at[off], device(source),
        ).wait_recv()
        return carry

    with jax.named_scope("arrivals"):
        lax.fori_loop(1, count, finish, 0)
    with jax.named_scope("combine"):
        combined = dot(weigh_ref[...], returned[...])
        for half in range(2):
            cols = slice(half * HALF, (half + 1) * HALF)
            span = slice(half * tokens, (half + 1) * tokens)
            out_ref[:, cols] = (stream_ref[:, cols].astype(F32) + combined[span, :]).astype(BF16)


def in_vmem(n):
    return [pl.BlockSpec(memory_space=pltpu.VMEM)] * n


def shards(
    nx, ny,
    query_proj, key_proj, value_proj, init_state, residual, out_gain, proj_weight, moe_gain,
    w_gate, w_up, w_down, expert_ids, gate_weights,
):
    tok, width = query_proj.shape[1:]
    heads = width // HD
    part = heads // nx
    token_rows = residual.shape[1]
    count = nx * ny * 2
    slots = count * BLK

    stacked = jnp.concatenate([w_gate[0], w_up[0], w_down[0]], axis=0)
    w_full = lax.all_gather(stacked, "expert", axis=1, tiled=True)

    state = (part, HD, HD)
    nz = lax.axis_size("expert")
    depth, shard = proj_weight.shape
    dma = pltpu.SemaphoreType.DMA
    stream, weighing, incoming = pl.pallas_call(
        functools.partial(front_kernel, nx, ny, nz),
        out_shape=[
            jax.ShapeDtypeStruct((token_rows, D), BF16),
            jax.ShapeDtypeStruct((2 * token_rows, slots), BF16),
            jax.ShapeDtypeStruct((slots, HALF), BF16),
        ],
        in_specs=in_vmem(10),
        out_specs=[*in_vmem(2), pl.BlockSpec(memory_space=pl.ANY)],
        scratch_shapes=[
            pltpu.VMEM((nx, *state), BF16),
            pltpu.VMEM((nx, *state), BF16),
            pltpu.VMEM(state, BF16),
            pltpu.VMEM((ny, *state), BF16),
            pltpu.VMEM((nx, *state), BF16),
            pltpu.VMEM((nx, *state), BF16),
            pltpu.VMEM((tok, width), F32),
            pltpu.VMEM((tok, width), BF16),
            pltpu.VMEM((nz, depth, shard), BF16),
            pltpu.VMEM((tok, D), F32),
            pltpu.VMEM((token_rows, D), BF16),
            pltpu.VMEM((token_rows, D), BF16),
            pltpu.VMEM((2 * token_rows, slots), BF16),
            pltpu.VMEM((2 * token_rows, HALF), BF16),
            pltpu.VMEM((slots, HALF), BF16),
            *[dma((n,)) for n in (nx, nx, ny, ny, nx, nx, nz, nz, ny, ny, ny, ny, ny, ny, ny, ny, 2)],
            dma,
            dma((count,)),
            dma((count,)),
        ],
        compiler_params=pltpu.CompilerParams(
            collective_id=0, has_side_effects=True, vmem_limit_bytes=VMEM_LIMIT
        ),
        cost_estimate=pl.CostEstimate(flops=10**9, bytes_accessed=3 * 10**8, transcendentals=0),
        name="front",
    )(
        query_proj[0], key_proj[0], value_proj[0], init_state[0], out_gain[None, :], proj_weight,
        residual[0], moe_gain[None, :], expert_ids[0], gate_weights[0],
    )

    out = pl.pallas_call(
        expert_kernel,
        out_shape=jax.ShapeDtypeStruct((token_rows, D), BF16),
        in_specs=in_vmem(4),
        out_specs=pl.BlockSpec(memory_space=pltpu.VMEM),
        scratch_shapes=[
            pltpu.VMEM((slots, HALF), BF16),
            pltpu.VMEM((slots, HALF), BF16),
            pltpu.SemaphoreType.DMA,
            pltpu.SemaphoreType.DMA((count,)),
            pltpu.SemaphoreType.DMA((count,)),
        ],
        compiler_params=pltpu.CompilerParams(
            collective_id=2, has_side_effects=True, vmem_limit_bytes=VMEM_LIMIT
        ),
        cost_estimate=pl.CostEstimate(flops=5 * 10**9, bytes_accessed=2 * 10**8, transcendentals=0),
        name="experts",
    )(incoming, w_full, stream, weighing)
    return out[None]


def solution(mesh):
    placed = (
        P("expert", "seq", "head"),
        P("expert", "seq", "head"),
        P("expert", "seq", "head"),
        P("expert", "head", None, None),
        P("expert", ("seq", "head"), None),
        P("head"),
        P("head", "expert"),
        P(),
        P(("seq", "head"), None, "expert"),
        P(("seq", "head"), None, "expert"),
        P(("seq", "head"), None, "expert"),
        P("expert", ("seq", "head"), None),
        P("expert", ("seq", "head"), None),
    )
    nx, ny = grid_of(mesh.shape["seq"])
    return jax.shard_map(
        functools.partial(shards, nx, ny),
        mesh=mesh,
        in_specs=placed,
        out_specs=P("expert", ("seq", "head"), None),
        check_vma=False,
    )
```

```python
import functools

import jax
import jax.numpy as jnp
from jax import lax
from jax.experimental import pallas as pl
from jax.experimental.pallas import tpu as pltpu
from jax.sharding import PartitionSpec as P

D = 2048
HALF = 1024
HD = 128
TOP = 6
CAP = 8
BLK = 2 * CAP
MESH = pl.DeviceIdType.MESH
BF16 = jnp.bfloat16
F32 = jnp.float32
CHUNKS = 2
VMEM_LIMIT = 56 * 2**20


def grid_of(seq):
    nx = 4 if seq == 32 else 2
    return nx, seq // nx


def dot(a, b, dims=((1,), (0,))):
    return lax.dot_general(a, b, (dims, ((), ())), preferred_element_type=F32)


def rows(index, size):
    return pl.ds(pl.multiple_of(index * size, size), size)


def remote(src, dst, send, recv, target):
    return pltpu.make_async_remote_copy(
        src_ref=src, dst_ref=dst, send_sem=send, recv_sem=recv, device_id=target, device_id_type=MESH
    )


def position(dy, ny):
    if dy == 0:
        return ny - 1
    return ny - 2 * dy if dy <= ny // 2 else 2 * dy - ny - 1


def place(ids_ref, gates_ref, weighing):
    tokens = ids_ref.shape[0]
    groups, _, group = weighing.shape
    slots = groups * group
    experts = slots // BLK
    expert = lax.broadcasted_iota(jnp.int32, (tokens, experts), 1)
    chosen = jnp.zeros((tokens, experts), F32)
    gates = jnp.zeros((tokens, experts), F32)
    for k in range(TOP):
        match = ids_ref[:, k : k + 1] == expert
        chosen = chosen + jnp.where(match, 1.0, 0.0)
        gates = gates + jnp.where(match, gates_ref[:, k : k + 1], 0.0)
    earlier = lax.broadcasted_iota(jnp.int32, (tokens, tokens), 1) < lax.broadcasted_iota(
        jnp.int32, (tokens, tokens), 0
    )
    earlier = jnp.where(earlier, 1.0, 0.0).astype(BF16)
    order = dot(earlier, chosen.astype(BF16))
    turn = (chosen * (order + 1.0)).astype(BF16)
    spread = lax.broadcasted_iota(jnp.int32, (experts, slots), 1) // BLK == lax.broadcasted_iota(
        jnp.int32, (experts, slots), 0
    )
    spread = jnp.where(spread, 1.0, 0.0).astype(BF16)
    turn = dot(turn, spread)
    gates = dot(gates.astype(BF16), spread)
    slot = lax.broadcasted_iota(jnp.int32, (tokens, slots), 1)
    place_in = lax.rem(slot, BLK)
    for half in range(2):
        wanted = (place_in - (half * CAP - 1)).astype(F32)
        hit = (turn == wanted) & (place_in // CAP == half)
        weights = jnp.where(hit, gates, 0.0).astype(BF16)
        for i in range(groups):
            weighing[i, half * tokens : (half + 1) * tokens, :] = weights[:, i * group : (i + 1) * group]


def front_kernel(
    nx, ny, nz, q_ref, k_ref, v_ref, init_ref, out_gain_ref, wo_ref, res_ref, gain_ref, ids_ref, gates_ref,
    stream_ref, weigh_ref, incoming_ref,
    loc, xin, tot, yin, pre, pin, att, mixed, wo, proj, snd, rcv, own_weighing, weighing, feats, outgoing,
    x_send, x_recv, y_send, y_recv, p_send, p_recv, wz_send, wz_recv, wy_send, wy_recv,
    right_send, right_recv, left_send, left_recv, pass_send, pass_recv, h_sem, g_send, g_recv, own_sem,
    f_send, f_recv, send, recv,
):
    s, h, z = lax.axis_index("seq"), lax.axis_index("head"), lax.axis_index("expert")
    y, x = s // nx, lax.rem(s, nx)
    across = 2 * nx
    sub = x * 2 + h
    heads = q_ref.shape[1] // HD
    part = heads // nx
    tokens = res_ref.shape[0]
    depth = wo_ref.shape[0] // (nx * ny)
    width = wo_ref.shape[1]

    def at_sub(k):
        other = lax.rem(sub + k, across)
        return (y * nx + other // 2, lax.rem(other, 2), z)

    def at_x(d):
        return (y * nx + lax.rem(x + d, nx), h, z)

    def at_y(d):
        return (lax.rem(y + d, ny) * nx + x, h, z)

    def at_z(d):
        return (s, h, lax.rem(z + d, nz))

    barrier = pltpu.get_barrier_semaphore()
    peers = [at_z(d) for d in range(1, nz)]
    peers += [at_y(d) for d in range(1, ny)]
    peers += [at_sub(d) for d in range(1, across)]
    for peer in peers:
        pl.semaphore_signal(barrier, inc=1, device_id=peer, device_id_type=MESH)
    with jax.named_scope("states"):
        for i in range(heads):
            cols = slice(i * HD, (i + 1) * HD)
            loc[i // part, i % part] = dot(k_ref[:, cols], v_ref[:, cols], ((0,), (0,))).astype(BF16)
    with jax.named_scope("barrier"):
        pl.semaphore_wait(barrier, len(peers))

    first = [
        remote(loc.at[lax.rem(x + d, nx)], xin.at[d], x_send.at[d], x_recv.at[d], at_x(d))
        for d in range(1, nx)
    ]
    for copy in first:
        copy.start()

    def strip(dx, dy):
        return pl.ds(
            pl.multiple_of((lax.rem(x + dx, nx) * ny + lax.rem(y + dy, ny)) * depth, depth), depth
        )

    mine = strip(0, 0)

    def fetch(d, owner):
        return remote(
            wo_ref.at[mine, :], wo.at[owner, mine, :], wz_send.at[d], wz_recv.at[d], at_z(d)
        )

    for d in range(1, nz):
        fetch(d, z).start()

    def along_y(b, step):
        block = wo.at[:, strip(0, ny - b), :]
        arrives = (b + step) % ny
        return remote(block, block, wy_send.at[arrives], wy_recv.at[arrives], at_y(step))

    def landed_y(b, step):
        block = wo.at[:, strip(0, ny - b), :]
        return remote(block, block, wy_send.at[b], wy_recv.at[b], at_y(step))

    def along_x(b, dx, sends, recvs, step):
        block = wo.at[:, strip(dx, ny - b), :]
        return remote(block, block, sends.at[b], recvs.at[b], at_x(step))

    reach = ny // 2
    to_right = [0, *range(reach + 1, ny)]

    def spread(b):
        along_x(b, 0, right_send, right_recv, 1).start()
        along_x(b, 0, left_send, left_recv, nx - 1).start()

    def relay_y(b):
        if b <= reach:
            landed_y(b, 1).wait_recv()
            if b < reach:
                along_y(b, 1).start()
        else:
            landed_y(b, ny - 1).wait_recv()
            if b > reach + 1:
                along_y(b, ny - 1).start()
        spread(b)

    def relay_x(b):
        if b in to_right:
            along_x(b, nx - 1, right_send, right_recv, 1).wait_recv()
            along_x(b, nx - 1, pass_send, pass_recv, 1).start()
        else:
            along_x(b, 1, left_send, left_recv, nx - 1).wait_recv()
            along_x(b, 1, pass_send, pass_recv, nx - 1).start()

    with jax.named_scope("states_x"):
        xin[0] = loc[x]
        for copy in first:
            copy.wait_recv()
    tot[...] = sum(xin[d].astype(F32) for d in range(nx)).astype(BF16)
    second = [remote(tot, yin.at[d], y_send.at[d], y_recv.at[d], at_y(d)) for d in range(1, ny)]
    for copy in second:
        copy.start()

    with jax.named_scope("fetched"):
        wo[z, mine, :] = wo_ref[mine, :]
        for d in range(1, nz):
            fetch(d, lax.rem(z + nz - d, nz)).wait_recv()
    along_y(0, 1).start()
    along_y(0, ny - 1).start()
    spread(0)

    with jax.named_scope("inner"):
        positions = q_ref.shape[0]
        causal = lax.broadcasted_iota(jnp.int32, (positions, positions), 0) >= lax.broadcasted_iota(
            jnp.int32, (positions, positions), 1
        )
        for i in range(heads):
            cols = slice(i * HD, (i + 1) * HD)
            scores = dot(q_ref[:, cols], k_ref[:, cols], ((1,), (1,)))
            scores = jnp.where(causal, scores, 0.0).astype(BF16)
            att[:, cols] = dot(scores, v_ref[:, cols])
    with jax.named_scope("placing"):
        place(ids_ref, gates_ref, own_weighing)
        weighing[0] = own_weighing[y]
        shared = [
            remote(
                own_weighing.at[lax.rem(y + d, ny)], weighing.at[d], g_send.at[d], g_recv.at[d], at_y(d)
            )
            for d in range(1, ny)
        ]
        for copy in shared:
            copy.start()
    with jax.named_scope("relay_1"):
        relay_y(1)
        relay_y(ny - 1)
        relay_x(0)

    before = jnp.zeros(tot.shape, F32)
    with jax.named_scope("states_y"):
        for d in range(1, ny):
            second[d - 1].wait_recv()
            before = before + yin[d].astype(F32) * (d <= y).astype(F32)
    third = []
    for e in range(nx):
        target = lax.rem(x + e, nx)
        state = before
        for d in range(nx):
            source = lax.rem(x + nx - d, nx)
            state = state + xin[d].astype(F32) * (source < target).astype(F32)
        pre[e] = state.astype(BF16)
        if e:
            copy = remote(pre.at[e], pin.at[e], p_send.at[e], p_recv.at[e], at_x(e))
            copy.start()
            third.append(copy)
    pin[0] = pre[0]
    with jax.named_scope("relay_2"):
        for step in range(2, reach):
            relay_y(step)
            relay_y(ny - step)
            relay_x(step - 1)
            relay_x(ny - step + 1)
        relay_y(reach)
        relay_x(reach - 1)
        relay_x(reach + 1)
    with jax.named_scope("mix"):
        for e in range(nx):
            if e:
                third[e - 1].wait_recv()
            for j in range(part):
                head = lax.rem(x + nx - e, nx) * part + j
                cols = rows(head, HD)
                state = (init_ref[head] + pin[e, j].astype(F32)).astype(BF16)
                out = att[:, cols] + dot(q_ref[:, cols], state)
                inv = lax.rsqrt(jnp.mean(out * out, axis=1, keepdims=True) + 1e-05)
                mixed[:, cols] = (out * inv * out_gain_ref[:, cols]).astype(BF16)
    with jax.named_scope("relay_3"):
        relay_x(reach)
        for b in range(ny):
            if b in to_right:
                along_x(b, 1, left_send, left_recv, nx - 1).wait_recv()
                along_x(b, 2, pass_send, pass_recv, 1).wait_recv()
            else:
                along_x(b, nx - 1, right_send, right_recv, 1).wait_recv()
                along_x(b, 2, pass_send, pass_recv, nx - 1).wait_recv()

    with jax.named_scope("project"):
        for c in range(nz):
            proj[:, c * width : (c + 1) * width] = dot(mixed[...], wo[c])
    snd[...] = proj[rows(1 - h, tokens), :].astype(BF16)
    half = remote(snd, rcv, h_sem.at[0], h_sem.at[1], (s, 1 - h, z))
    half.start()
    for copy in first + second + third:
        copy.wait_send()
    for d in range(1, nz):
        fetch(d, z).wait_send()
    for b in range(ny):
        along_x(b, 0, right_send, right_recv, 1).wait_send()
        along_x(b, 0, left_send, left_recv, nx - 1).wait_send()
        if b in to_right:
            along_x(b, nx - 1, pass_send, pass_recv, 1).wait_send()
        else:
            along_x(b, 1, pass_send, pass_recv, nx - 1).wait_send()
        if b and b <= reach:
            along_y(b - 1, 1).wait_send()
        elif b:
            along_y((b + 1) % ny, ny - 1).wait_send()
    with jax.named_scope("other_half"):
        half.wait_recv()
    stream = (
        res_ref[...].astype(F32) + (proj[rows(h, tokens), :] + rcv[...].astype(F32))
    ).astype(BF16)
    stream_ref[...] = stream
    stream_f = stream.astype(F32)
    inv = lax.rsqrt(jnp.mean(stream_f * stream_f, axis=1, keepdims=True) + 1e-06)
    moe_in = (stream_f * inv * gain_ref[...]).astype(BF16)
    chunks, wide = feats.shape[1], feats.shape[3]
    for c in range(chunks):
        feats[0, c, :tokens, :] = moe_in[:, c * wide : (c + 1) * wide]
        feats[0, c, tokens:, :] = moe_in[:, HALF + c * wide : HALF + (c + 1) * wide]

    def ring(b, c, step):
        arrives = (b + step) % ny
        sem = arrives * chunks + c
        return remote(
            feats.at[b, c], feats.at[arrives, c], f_send.at[sem], f_recv.at[sem], at_y(step)
        )

    for c in range(chunks):
        ring(0, c, 1).start()
        ring(0, c, ny - 1).start()
    for d in range(1, ny):
        shared[d - 1].wait_recv()
    weigh_ref[...] = weighing[...]

    def block(b, k):
        other = lax.rem(sub + k, across)
        slot = position((ny - b) % ny, ny) * across + sub
        sem = b * across + k
        return remote(
            outgoing.at[rows(b * across + other, BLK), :], incoming_ref.at[rows(slot, BLK), :],
            send.at[sem], recv.at[sem], at_sub(k),
        )

    def arrived(b, k):
        other = lax.rem(sub + across - k, across)
        slot = position((ny - b) % ny, ny) * across + other
        sem = b * across + k
        return remote(
            outgoing.at[rows(b * across + other, BLK), :], incoming_ref.at[rows(slot, BLK), :],
            send.at[sem], recv.at[sem], at_sub(k),
        )

    def keep(b):
        slot = position((ny - b) % ny, ny) * across + sub
        return pltpu.make_async_copy(
            outgoing.at[rows(b * across + sub, BLK), :], incoming_ref.at[rows(slot, BLK), :], own_sem.at[b]
        )

    group = across * BLK
    around = [0]
    for step in range(1, reach):
        around += [step, ny - step]
    around.append(reach)
    for b in around:
        picks = jnp.where(weighing[b].astype(F32) > 0.0, 1.0, 0.0).astype(BF16)
        step = 1 if b <= reach else ny - 1
        for c in range(chunks):
            if b:
                ring((b - step) % ny, c, step).wait_recv()
                if b not in (reach, reach + 1):
                    ring(b, c, step).start()
            outgoing[b * group : (b + 1) * group, c * wide : (c + 1) * wide] = dot(
                picks, feats[b, c], ((0,), (0,))
            ).astype(BF16)

        def begin(k, carry, b=b):
            block(b, k).start()
            return carry

        lax.fori_loop(1, across, begin, 0)
        keep(b).start()

    half.wait_send()
    for copy in shared:
        copy.wait_send()
    for b in range(1, ny):
        step = 1 if b <= reach else ny - 1
        for c in range(chunks):
            ring((b - step) % ny, c, step).wait_send()
    for b in around:
        keep(b).wait()

        def finish(k, carry, b=b):
            block(b, k).wait_send()
            arrived(b, k).wait_recv()
            return carry

        lax.fori_loop(1, across, finish, 0)


def expert_kernel(
    nx, ny, x_ref, w_ref, stream_ref, weigh_ref, out_ref, results, returned, right_out, right_in, left_out, left_in,
    send, recv, right_send, right_recv, left_send, left_recv,
):
    s, h, z = lax.axis_index("seq"), lax.axis_index("head"), lax.axis_index("expert")
    y, x = s // nx, lax.rem(s, nx)
    across = 2 * nx
    sub = x * 2 + h
    reach = ny // 2
    group = across * BLK
    tokens = stream_ref.shape[0]
    hidden_width = w_ref.shape[0] // 3
    chunks, wide = right_out.shape[1], right_out.shape[3]

    def at_sub(k):
        other = lax.rem(sub + k, across)
        return (y * nx + other // 2, lax.rem(other, 2), z)

    def at_y(d):
        return (lax.rem(y + d, ny) * nx + x, h, z)

    barrier = pltpu.get_barrier_semaphore()
    peers = [at_y(1), at_y(ny - 1), *[at_sub(k) for k in range(1, across)]]
    for peer in peers:
        pl.semaphore_signal(barrier, inc=1, device_id=peer, device_id_type=MESH)

    def block(p, k, source):
        slot = p * across + lax.rem(sub + k, across)
        sem = p * across + k
        return remote(
            results.at[rows(slot, BLK), :], returned.at[rows(p * across + source, BLK), :],
            send.at[sem], recv.at[sem], at_sub(k),
        )

    def compute(g):
        span = slice(2 * g * group, 2 * (g + 1) * group)
        blocks = x_ref[span, :].astype(F32).reshape(2 * across, BLK, HALF)
        low = blocks[:, :CAP].reshape(2 * across * CAP, HALF).astype(BF16)
        high = blocks[:, CAP:].reshape(2 * across * CAP, HALF).astype(BF16)
        acts = []
        for i in range(2):
            part = slice(i * hidden_width, (i + 1) * hidden_width)
            acts.append(
                dot(low, w_ref[part, :HALF], ((1,), (1,)))
                + dot(high, w_ref[part, HALF:], ((1,), (1,)))
            )
        gate, up = acts
        hidden = (gate / (1.0 + jnp.exp(-gate)) * up).astype(BF16)
        outs = [
            dot(hidden, w_ref[2 * hidden_width :, i * HALF : (i + 1) * HALF]).reshape(
                2 * across, CAP, HALF
            )
            for i in range(2)
        ]
        results[span, :] = (
            jnp.concatenate(outs, axis=1).reshape(2 * across * BLK, HALF).astype(BF16)
        )
        if g == 0:
            pl.semaphore_wait(barrier, len(peers))
        for p in (2 * g, 2 * g + 1):

            def begin(k, carry, p=p):
                block(p, k, sub).start()
                return carry

            lax.fori_loop(1, across, begin, 0)
            own = rows(p * across + sub, BLK)
            returned[own, :] = results[own, :]

    def landed(p):
        def one(k, carry):
            block(p, k, lax.rem(sub + across - k, across)).wait_recv()
            return carry

        lax.fori_loop(1, across, one, 0)

    def weighed(dy, c):
        p = position(dy, ny)
        return dot(
            weigh_ref[(ny - dy) % ny],
            returned[p * group : (p + 1) * group, c * wide : (c + 1) * wide],
        )

    def to_right(step, c):
        sem = step * chunks + c
        return remote(
            right_out.at[step, c], right_in.at[step, c], right_send.at[sem], right_recv.at[sem], at_y(1)
        )

    def to_left(step, c):
        sem = step * chunks + c
        return remote(
            left_out.at[step, c], left_in.at[step, c], left_send.at[sem], left_recv.at[sem], at_y(ny - 1)
        )

    def advance(step):
        for dy, to, outbox, inbox in (
            (reach - step, to_right, right_out, right_in),
            (reach + 1 + step, to_left, left_out, left_in),
        ):
            if dy == ny:
                continue
            landed(position(dy, ny))
            for c in range(chunks):
                total = weighed(dy, c)
                if step:
                    to(step - 1, c).wait_recv()
                    total = total + inbox[step - 1, c].astype(F32)
                outbox[step, c] = total.astype(BF16)
                to(step, c).start()

    for g in range(ny // 2):
        compute(g)
        if g:
            advance(g - 1)
    for step in range(ny // 2 - 1, reach):
        advance(step)
    landed(ny - 1)
    for c in range(chunks):
        total = weighed(0, c)
        to_right(reach - 1, c).wait_recv()
        to_left(reach - 2, c).wait_recv()
        total = total + right_in[reach - 1, c].astype(F32) + left_in[reach - 2, c].astype(F32)
        for half in range(2):
            cols = slice(half * HALF + c * wide, half * HALF + (c + 1) * wide)
            out_ref[:, cols] = (
                stream_ref[:, cols].astype(F32) + total[half * tokens : (half + 1) * tokens, :]
            ).astype(BF16)
    for c in range(chunks):
        for step in range(reach):
            to_right(step, c).wait_send()
        for step in range(reach - 1):
            to_left(step, c).wait_send()
    for p in range(ny):

        def finish(k, carry, p=p):
            block(p, k, sub).wait_send()
            return carry

        lax.fori_loop(1, across, finish, 0)


def in_vmem(n):
    return [pl.BlockSpec(memory_space=pltpu.VMEM)] * n


def shards(
    nx, ny,
    query_proj, key_proj, value_proj, init_state, residual, out_gain, proj_weight, moe_gain,
    w_gate, w_up, w_down, expert_ids, gate_weights,
):
    tok, width = query_proj.shape[1:]
    heads = width // HD
    part = heads // nx
    token_rows = residual.shape[1]
    count = nx * ny * 2
    slots = count * BLK
    group = 2 * nx * BLK

    stacked = jnp.concatenate([w_gate[0], w_up[0], w_down[0]], axis=0)
    w_full = lax.all_gather(stacked, "expert", axis=1, tiled=True)

    state = (part, HD, HD)
    nz = lax.axis_size("expert")
    depth, shard = proj_weight.shape
    dma = pltpu.SemaphoreType.DMA
    stream, weighing, incoming = pl.pallas_call(
        functools.partial(front_kernel, nx, ny, nz),
        out_shape=[
            jax.ShapeDtypeStruct((token_rows, D), BF16),
            jax.ShapeDtypeStruct((ny, 2 * token_rows, group), BF16),
            jax.ShapeDtypeStruct((slots, HALF), BF16),
        ],
        in_specs=in_vmem(10),
        out_specs=[*in_vmem(2), pl.BlockSpec(memory_space=pl.ANY)],
        scratch_shapes=[
            pltpu.VMEM((nx, *state), BF16),
            pltpu.VMEM((nx, *state), BF16),
            pltpu.VMEM(state, BF16),
            pltpu.VMEM((ny, *state), BF16),
            pltpu.VMEM((nx, *state), BF16),
            pltpu.VMEM((nx, *state), BF16),
            pltpu.VMEM((tok, width), F32),
            pltpu.VMEM((tok, width), BF16),
            pltpu.VMEM((nz, depth, shard), BF16),
            pltpu.VMEM((tok, D), F32),
            pltpu.VMEM((token_rows, D), BF16),
            pltpu.VMEM((token_rows, D), BF16),
            pltpu.VMEM((ny, 2 * token_rows, group), BF16),
            pltpu.VMEM((ny, 2 * token_rows, group), BF16),
            pltpu.VMEM((ny, CHUNKS, 2 * token_rows, HALF // CHUNKS), BF16),
            pltpu.VMEM((slots, HALF), BF16),
            *[dma((n,)) for n in (nx, nx, ny, ny, nx, nx, nz, nz, ny, ny, ny, ny, ny, ny, ny, ny, 2)],
            *[dma((n,)) for n in (ny, ny, ny, ny * CHUNKS, ny * CHUNKS, count, count)],
        ],
        compiler_params=pltpu.CompilerParams(
            collective_id=0, has_side_effects=True, vmem_limit_bytes=VMEM_LIMIT
        ),
        cost_estimate=pl.CostEstimate(flops=10**9, bytes_accessed=3 * 10**8, transcendentals=0),
        name="front",
    )(
        query_proj[0], key_proj[0], value_proj[0], init_state[0], out_gain[None, :], proj_weight,
        residual[0], moe_gain[None, :], expert_ids[0], gate_weights[0],
    )

    passing = (CHUNKS, 2 * token_rows, HALF // CHUNKS)
    out = pl.pallas_call(
        functools.partial(expert_kernel, nx, ny),
        out_shape=jax.ShapeDtypeStruct((token_rows, D), BF16),
        in_specs=in_vmem(4),
        out_specs=pl.BlockSpec(memory_space=pltpu.VMEM),
        scratch_shapes=[
            pltpu.VMEM((slots, HALF), BF16),
            pltpu.VMEM((slots, HALF), BF16),
            *[pltpu.VMEM((n, *passing), BF16) for n in (ny // 2, ny // 2, ny // 2 - 1, ny // 2 - 1)],
            *[dma((n,)) for n in (count, count)],
            *[dma((n * CHUNKS,)) for n in (ny // 2, ny // 2, ny // 2 - 1, ny // 2 - 1)],
        ],
        compiler_params=pltpu.CompilerParams(
            collective_id=2, has_side_effects=True, vmem_limit_bytes=VMEM_LIMIT
        ),
        cost_estimate=pl.CostEstimate(flops=5 * 10**9, bytes_accessed=2 * 10**8, transcendentals=0),
        name="experts",
    )(incoming, w_full, stream, weighing)
    return out[None]


def solution(mesh):
    placed = (
        P("expert", "seq", "head"),
        P("expert", "seq", "head"),
        P("expert", "seq", "head"),
        P("expert", "head", None, None),
        P("expert", ("seq", "head"), None),
        P("head"),
        P("head", "expert"),
        P(),
        P(("seq", "head"), None, "expert"),
        P(("seq", "head"), None, "expert"),
        P(("seq", "head"), None, "expert"),
        P("expert", ("seq", "head"), None),
        P("expert", ("seq", "head"), None),
    )
    nx, ny = grid_of(mesh.shape["seq"])
    return jax.shard_map(
        functools.partial(shards, nx, ny),
        mesh=mesh,
        in_specs=placed,
        out_specs=P("expert", ("seq", "head"), None),
        check_vma=False,
    )
```

```python
import functools

import jax
import jax.numpy as jnp
from jax import lax
from jax.experimental import pallas as pl
from jax.experimental.pallas import tpu as pltpu
from jax.sharding import PartitionSpec as P

D = 2048
HALF = 1024
HD = 128
TOP = 6
CAP = 8
BLK = 2 * CAP
MESH = pl.DeviceIdType.MESH
BF16 = jnp.bfloat16
F32 = jnp.float32
CHUNKS = 2
VMEM_LIMIT = 56 * 2**20


def grid_of(seq):
    nx = 4 if seq == 32 else 2
    return nx, seq // nx


def dot(a, b, dims=((1,), (0,))):
    return lax.dot_general(a, b, (dims, ((), ())), preferred_element_type=F32)


def rows(index, size):
    return pl.ds(pl.multiple_of(index * size, size), size)


def remote(src, dst, send, recv, target):
    return pltpu.make_async_remote_copy(
        src_ref=src, dst_ref=dst, send_sem=send, recv_sem=recv, device_id=target, device_id_type=MESH
    )


def position(dy, ny):
    if dy == 0:
        return ny - 1
    return ny - 2 * dy if dy <= ny // 2 else 2 * dy - ny - 1


def way(b, c, n):
    return 1 if b < n // 2 or (b == n // 2 and c == 0) else n - 1


def onward(b, c, n):
    step = way(b, c, n)
    further = (b + step) % n
    return step if further and way(further, c, n) == step else None


def place(ids_ref, gates_ref, weighing):
    tokens = ids_ref.shape[2]
    groups, _, group = weighing.shape
    slots = groups * group
    experts = slots // BLK
    expert = lax.broadcasted_iota(jnp.int32, (experts, tokens), 0)
    chosen = jnp.zeros((experts, tokens), F32)
    gates = jnp.zeros((experts, tokens), F32)
    for k in range(TOP):
        match = ids_ref[k] == expert
        chosen = chosen + jnp.where(match, 1.0, 0.0)
        gates = gates + jnp.where(match, gates_ref[k], 0.0)
    earlier = lax.broadcasted_iota(jnp.int32, (tokens, tokens), 0) < lax.broadcasted_iota(
        jnp.int32, (tokens, tokens), 1
    )
    earlier = jnp.where(earlier, 1.0, 0.0).astype(BF16)
    order = dot(chosen.astype(BF16), earlier)
    turn = (chosen * (order + 1.0)).astype(BF16)
    spread = lax.broadcasted_iota(jnp.int32, (experts, slots), 1) // BLK == lax.broadcasted_iota(
        jnp.int32, (experts, slots), 0
    )
    spread = jnp.where(spread, 1.0, 0.0).astype(BF16)
    turn = dot(turn, spread, ((0,), (0,)))
    gates = dot(gates.astype(BF16), spread, ((0,), (0,)))
    slot = lax.broadcasted_iota(jnp.int32, (tokens, slots), 1)
    place_in = lax.rem(slot, BLK)
    for half in range(2):
        wanted = (place_in - (half * CAP - 1)).astype(F32)
        hit = (turn == wanted) & (place_in // CAP == half)
        weights = jnp.where(hit, gates, 0.0).astype(BF16)
        for i in range(groups):
            weighing[i, half * tokens : (half + 1) * tokens, :] = weights[:, i * group : (i + 1) * group]


def front_kernel(
    nx, ny, nz, q_ref, k_ref, v_ref, init_ref, out_gain_ref, wo_ref, res_ref, gain_ref, ids_ref, gates_ref, gate_ref, up_ref, down_ref,
    stream_ref, weigh_ref, incoming_ref, gate_full_ref, up_full_ref, down_full_ref,
    loc, xin, tot, yin, pre, pin, att, mixed, wo, proj, snd, rcv, own_weighing, weighing, feats, outgoing,
    x_send, x_recv, y_send, y_recv, p_send, p_recv, wz_send, wz_recv, wy_send, wy_recv,
    right_send, right_recv, left_send, left_recv, pass_send, pass_recv, h_sem, g_send, g_recv, own_sem,
    f_send, f_recv, send, recv, bx_send, bx_recv, by_send, by_recv, ring_send, ring_recv, ring_own,
):
    s, h, z = lax.axis_index("seq"), lax.axis_index("head"), lax.axis_index("expert")
    y, x = s // nx, lax.rem(s, nx)
    across = 2 * nx
    sub = x * 2 + h
    heads = q_ref.shape[1] // HD
    part = heads // nx
    tokens = res_ref.shape[0]
    depth, width = wo.shape[3:]
    reach = ny // 2
    cross = 6 * nz // 8

    def at_sub(k):
        other = lax.rem(sub + k, across)
        return (y * nx + other // 2, lax.rem(other, 2), z)

    def at_x(d):
        return (y * nx + lax.rem(x + d, nx), h, z)

    def at_y(d):
        return (lax.rem(y + d, ny) * nx + x, h, z)

    def at_z(d):
        return (s, h, lax.rem(z + d, nz))

    barrier = pltpu.get_barrier_semaphore()
    peers = [at_z(d) for d in range(1, nz)]
    peers += [at_y(d) for d in range(1, ny)]
    peers += [at_sub(d) for d in range(1, across)]
    for peer in peers:
        pl.semaphore_signal(barrier, inc=1, device_id=peer, device_id_type=MESH)
    with jax.named_scope("states"):
        for i in range(heads):
            cols = slice(i * HD, (i + 1) * HD)
            loc[i // part, i % part] = dot(k_ref[:, cols], v_ref[:, cols], ((0,), (0,))).astype(BF16)
    with jax.named_scope("barrier"):
        pl.semaphore_wait(barrier, len(peers))

    first = [
        remote(loc.at[lax.rem(x + d, nx)], xin.at[d], x_send.at[d], x_recv.at[d], at_x(d))
        for d in range(1, nx)
    ]
    for copy in first:
        copy.start()

    shares = (gate_ref, up_ref, down_ref)
    fulls = (gate_full_ref, up_full_ref, down_full_ref)
    pieces = 2 * len(shares)
    half_rows = gate_ref.shape[0] // 2

    def piece(b, i, step):
        span = pl.ds(i % 2 * half_rows, half_rows)
        there = fulls[i // 2].at[lax.rem(z + nz - b, nz), span, :]
        sem = (b + step) % nz * pieces + i
        return remote(
            there if b else shares[i // 2].at[span, :], there, ring_send.at[sem], ring_recv.at[sem], at_z(step)
        )

    def piece_came(b, i):
        span = pl.ds(i % 2 * half_rows, half_rows)
        there = fulls[i // 2].at[lax.rem(z + nz - b, nz), span, :]
        sem = b * pieces + i
        return remote(there, there, ring_send.at[sem], ring_recv.at[sem], at_z(1))

    def relay_ring(distance, later):
        for i in range(later * pieces // 2, (later + 1) * pieces // 2):
            for b in sorted({distance, nz - distance}):
                piece_came(b, i).wait_recv()
                step = onward(b, later, nz)
                if step:
                    piece(b, i, step).start()

    mine = rows(x * ny + y, depth)

    def fetch(d, owner):
        return remote(
            wo_ref.at[mine, :], wo.at[owner, x, y], wz_send.at[d], wz_recv.at[d], at_z(d)
        )

    for d in range(1, nz):
        fetch(d, z).start()
    for i in range(pieces):
        for step in (1, nz - 1):
            piece(0, i, step).start()
    kept = [
        pltpu.make_async_copy(share, full.at[z], ring_own.at[i])
        for i, (share, full) in enumerate(zip(shares, fulls, strict=True))
    ]
    for copy in kept:
        copy.start()

    def chip(dx, b):
        return wo.at[pl.ds(0, cross), lax.rem(x + dx, nx), lax.rem(y + ny - b, ny)]

    def along_y(b, step):
        arrives = (b + step) % ny
        return remote(chip(0, b), chip(0, b), wy_send.at[arrives], wy_recv.at[arrives], at_y(step))

    def landed_y(b):
        return remote(chip(0, b), chip(0, b), wy_send.at[b], wy_recv.at[b], at_y(1))

    def along_x(b, dx, sends, recvs, step):
        return remote(chip(dx, b), chip(dx, b), sends.at[b], recvs.at[b], at_x(step))

    rest = pl.ds(cross, nz - cross)

    def side(d):
        own = wo.at[rest, x, y]
        return remote(own, own, bx_send.at[d], bx_recv.at[d], at_x(d))

    def side_came(d):
        there = wo.at[rest, lax.rem(x + nx - d, nx), y]
        return remote(there, there, bx_send.at[d], bx_recv.at[d], at_x(d))

    def row(b, c, step):
        part_of = wo.at[rest, pl.ds(c * (nx // 2), nx // 2), lax.rem(y + ny - b, ny)]
        sem = (b + step) % ny * 2 + c
        return remote(part_of, part_of, by_send.at[sem], by_recv.at[sem], at_y(step))

    def row_came(b, c):
        there = wo.at[rest, pl.ds(c * (nx // 2), nx // 2), lax.rem(y + ny - b, ny)]
        sem = b * 2 + c
        return remote(there, there, by_send.at[sem], by_recv.at[sem], at_y(1))

    def relay_row(b):
        for c in range(2):
            row_came(b, c).wait_recv()
            step = onward(b, c, ny)
            if step:
                row(b, c, step).start()

    to_right = [0, *range(reach + 1, ny)]

    def spread(b):
        along_x(b, 0, right_send, right_recv, 1).start()
        along_x(b, 0, left_send, left_recv, nx - 1).start()

    def relay_y(b):
        landed_y(b).wait_recv()
        if b < reach:
            along_y(b, 1).start()
        elif b > reach + 1:
            along_y(b, ny - 1).start()
        spread(b)

    def relay_x(b):
        if b in to_right:
            along_x(b, nx - 1, right_send, right_recv, 1).wait_recv()
            along_x(b, nx - 1, pass_send, pass_recv, 1).start()
        else:
            along_x(b, 1, left_send, left_recv, nx - 1).wait_recv()
            along_x(b, 1, pass_send, pass_recv, nx - 1).start()

    with jax.named_scope("states_x"):
        xin[0] = loc[x]
        for copy in first:
            copy.wait_recv()
    tot[...] = sum(xin[d].astype(F32) for d in range(nx)).astype(BF16)
    second = [remote(tot, yin.at[d], y_send.at[d], y_recv.at[d], at_y(d)) for d in range(1, ny)]
    for copy in second:
        copy.start()

    with jax.named_scope("fetched"):
        wo[z, x, y] = wo_ref[mine, :]
        for d in range(1, nz):
            fetch(d, lax.rem(z + nz - d, nz)).wait_recv()
    along_y(0, 1).start()
    along_y(0, ny - 1).start()
    for d in range(1, nx):
        side(d).start()
    spread(0)

    with jax.named_scope("inner"):
        positions = q_ref.shape[0]
        causal = lax.broadcasted_iota(jnp.int32, (positions, positions), 0) >= lax.broadcasted_iota(
            jnp.int32, (positions, positions), 1
        )
        for i in range(heads):
            cols = slice(i * HD, (i + 1) * HD)
            scores = dot(q_ref[:, cols], k_ref[:, cols], ((1,), (1,)))
            scores = jnp.where(causal, scores, 0.0).astype(BF16)
            att[:, cols] = dot(scores, v_ref[:, cols])
    with jax.named_scope("placing"):
        place(ids_ref, gates_ref, own_weighing)
    with jax.named_scope("relay_1"):
        for d in range(1, nx):
            side_came(d).wait_recv()
        for c in range(2):
            for step in (1, ny - 1):
                row(0, c, step).start()
        relay_y(1)
        relay_y(ny - 1)
        relay_x(0)
        relay_row(1)
        relay_row(ny - 1)
        relay_ring(1, 0)

    before = jnp.zeros(tot.shape, F32)
    with jax.named_scope("states_y"):
        for d in range(1, ny):
            second[d - 1].wait_recv()
            before = before + yin[d].astype(F32) * (d <= y).astype(F32)
    third = []
    for e in range(nx):
        target = lax.rem(x + e, nx)
        state = before
        for d in range(nx):
            source = lax.rem(x + nx - d, nx)
            state = state + xin[d].astype(F32) * (source < target).astype(F32)
        pre[e] = state.astype(BF16)
        if e:
            copy = remote(pre.at[e], pin.at[e], p_send.at[e], p_recv.at[e], at_x(e))
            copy.start()
            third.append(copy)
    pin[0] = pre[0]
    with jax.named_scope("relay_2"):
        for step in range(2, reach):
            relay_y(step)
            relay_y(ny - step)
            relay_row(step)
            relay_row(ny - step)
            relay_x(step - 1)
            relay_x(ny - step + 1)
        relay_y(reach)
        relay_row(reach)
        relay_x(reach - 1)
        relay_x(reach + 1)
        relay_ring(1, 1)
    weighing[0] = own_weighing[y]
    shared = [
        remote(
            own_weighing.at[lax.rem(y + d, ny)], weighing.at[d], g_send.at[d], g_recv.at[d], at_y(d)
        )
        for d in range(1, ny)
    ]
    for copy in shared:
        copy.start()
    with jax.named_scope("mix"):
        for e in range(nx):
            if e:
                third[e - 1].wait_recv()
            for j in range(part):
                head = lax.rem(x + nx - e, nx) * part + j
                cols = rows(head, HD)
                state = (init_ref[head] + pin[e, j].astype(F32)).astype(BF16)
                out = att[:, cols] + dot(q_ref[:, cols], state)
                inv = lax.rsqrt(jnp.mean(out * out, axis=1, keepdims=True) + 1e-05)
                mixed[:, cols] = (out * inv * out_gain_ref[:, cols]).astype(BF16)
    with jax.named_scope("relay_3"):
        relay_x(reach)
        for b in range(ny):
            if b in to_right:
                along_x(b, 1, left_send, left_recv, nx - 1).wait_recv()
                along_x(b, 2, pass_send, pass_recv, 1).wait_recv()
            else:
                along_x(b, nx - 1, right_send, right_recv, 1).wait_recv()
                along_x(b, 2, pass_send, pass_recv, nx - 1).wait_recv()

    relay_ring(2, 0)
    with jax.named_scope("project"):
        for c in range(nz):
            proj[:, c * width : (c + 1) * width] = dot(mixed[...], wo[c].reshape(nx * ny * depth, width))
    snd[...] = proj[rows(1 - h, tokens), :].astype(BF16)
    half = remote(snd, rcv, h_sem.at[0], h_sem.at[1], (s, 1 - h, z))
    half.start()
    relay_ring(2, 1)
    for copy in first + second + third:
        copy.wait_send()
    for d in range(1, nz):
        fetch(d, z).wait_send()
    for b in range(ny):
        along_x(b, 0, right_send, right_recv, 1).wait_send()
        along_x(b, 0, left_send, left_recv, nx - 1).wait_send()
        if b in to_right:
            along_x(b, nx - 1, pass_send, pass_recv, 1).wait_send()
        else:
            along_x(b, 1, pass_send, pass_recv, nx - 1).wait_send()
        if b and b <= reach:
            along_y(b - 1, 1).wait_send()
        elif b:
            along_y((b + 1) % ny, ny - 1).wait_send()
        if b:
            for c in range(2):
                row_came(b, c).wait_send()
    for d in range(1, nx):
        side(d).wait_send()
    with jax.named_scope("other_half"):
        half.wait_recv()
    stream = (
        res_ref[...].astype(F32) + (proj[rows(h, tokens), :] + rcv[...].astype(F32))
    ).astype(BF16)
    stream_ref[...] = stream
    stream_f = stream.astype(F32)
    inv = lax.rsqrt(jnp.mean(stream_f * stream_f, axis=1, keepdims=True) + 1e-06)
    moe_in = (stream_f * inv * gain_ref[...]).astype(BF16)
    chunks, wide = feats.shape[1], feats.shape[3]
    for c in range(chunks):
        feats[0, c, :tokens, :] = moe_in[:, c * wide : (c + 1) * wide]
        feats[0, c, tokens:, :] = moe_in[:, HALF + c * wide : HALF + (c + 1) * wide]

    def ring(b, c, step):
        arrives = (b + step) % ny
        sem = arrives * chunks + c
        return remote(
            feats.at[b, c], feats.at[arrives, c], f_send.at[sem], f_recv.at[sem], at_y(step)
        )

    for c in range(chunks):
        ring(0, c, 1).start()
        ring(0, c, ny - 1).start()
    for d in range(1, ny):
        shared[d - 1].wait_recv()
    weigh_ref[...] = weighing[...]

    def block(b, k):
        other = lax.rem(sub + k, across)
        slot = position((ny - b) % ny, ny) * across + sub
        sem = b * across + k
        return remote(
            outgoing.at[rows(b * across + other, BLK), :], incoming_ref.at[rows(slot, BLK), :],
            send.at[sem], recv.at[sem], at_sub(k),
        )

    def arrived(b, k):
        other = lax.rem(sub + across - k, across)
        slot = position((ny - b) % ny, ny) * across + other
        sem = b * across + k
        return remote(
            outgoing.at[rows(b * across + other, BLK), :], incoming_ref.at[rows(slot, BLK), :],
            send.at[sem], recv.at[sem], at_sub(k),
        )

    def keep(b):
        slot = position((ny - b) % ny, ny) * across + sub
        return pltpu.make_async_copy(
            outgoing.at[rows(b * across + sub, BLK), :], incoming_ref.at[rows(slot, BLK), :], own_sem.at[b]
        )

    group = across * BLK
    around = [0]
    for step in range(1, reach):
        around += [step, ny - step]
    around.append(reach)
    for b in around:
        if b == 2:
            relay_ring(3, 0)
        if b == reach:
            relay_ring(3, 1)
        picks = jnp.where(weighing[b].astype(F32) > 0.0, 1.0, 0.0).astype(BF16)
        for c in range(chunks):
            if b:
                step = way(b, c, ny)
                ring((b - step) % ny, c, step).wait_recv()
                step = onward(b, c, ny)
                if step:
                    ring(b, c, step).start()
            outgoing[b * group : (b + 1) * group, c * wide : (c + 1) * wide] = dot(
                picks, feats[b, c], ((0,), (0,))
            ).astype(BF16)

        def begin(k, carry, b=b):
            block(b, k).start()
            return carry

        lax.fori_loop(1, across, begin, 0)
        keep(b).start()

    half.wait_send()
    for copy in shared:
        copy.wait_send()
    for b in range(1, ny):
        for c in range(chunks):
            step = way(b, c, ny)
            ring((b - step) % ny, c, step).wait_send()
    for later in range(2):
        relay_ring(nz // 2, later)
    for copy in kept:
        copy.wait()
    for b in range(1, nz):
        for i in range(pieces):
            piece_came(b, i).wait_send()
    for b in around:
        keep(b).wait()

        def finish(k, carry, b=b):
            block(b, k).wait_send()
            arrived(b, k).wait_recv()
            return carry

        lax.fori_loop(1, across, finish, 0)


def expert_kernel(
    nx, ny, x_ref, gate_ref, up_ref, down_ref, stream_ref, weigh_ref, out_ref, results, returned, right_out, right_in, left_out, left_in,
    send, recv, right_send, right_recv, left_send, left_recv,
):
    s, h, z = lax.axis_index("seq"), lax.axis_index("head"), lax.axis_index("expert")
    y, x = s // nx, lax.rem(s, nx)
    across = 2 * nx
    sub = x * 2 + h
    reach = ny // 2
    group = across * BLK
    tokens = stream_ref.shape[0]
    many = ny // 2
    shards_in_half = down_ref.shape[0] // 2
    chunks, wide = right_out.shape[1], right_out.shape[3]

    def at_sub(k):
        other = lax.rem(sub + k, across)
        return (y * nx + other // 2, lax.rem(other, 2), z)

    def at_y(d):
        return (lax.rem(y + d, ny) * nx + x, h, z)

    barrier = pltpu.get_barrier_semaphore()
    peers = [at_y(1), at_y(ny - 1), *[at_sub(k) for k in range(1, across)]]
    for peer in peers:
        pl.semaphore_signal(barrier, inc=1, device_id=peer, device_id_type=MESH)

    def block(p, k, source):
        slot = p * across + lax.rem(sub + k, across)
        sem = p * across + k
        return remote(
            results.at[rows(slot, BLK), :], returned.at[rows(p * across + source, BLK), :],
            send.at[sem], recv.at[sem], at_sub(k),
        )

    def compute(g):
        span = slice(many * g * group, many * (g + 1) * group)
        blocks = x_ref[span, :].astype(F32).reshape(many * across, BLK, HALF)
        low = blocks[:, :CAP].reshape(many * across * CAP, HALF).astype(BF16)
        high = blocks[:, CAP:].reshape(many * across * CAP, HALF).astype(BF16)
        acts = []
        for w_ref in (gate_ref, up_ref):
            total = None
            for i, values in enumerate((low, high)):
                for j in range(shards_in_half):
                    wide_in = HALF // shards_in_half
                    term = dot(
                        values[:, j * wide_in : (j + 1) * wide_in], w_ref[i * shards_in_half + j], ((1,), (1,))
                    )
                    total = term if total is None else total + term
            acts.append(total)
        gate, up = acts
        hidden = (gate / (1.0 + jnp.exp(-gate)) * up).astype(BF16)
        outs = [
            jnp.concatenate(
                [dot(hidden, down_ref[i * shards_in_half + j]) for j in range(shards_in_half)], axis=1
            ).reshape(many * across, CAP, HALF)
            for i in range(2)
        ]
        results[span, :] = (
            jnp.concatenate(outs, axis=1).reshape(many * across * BLK, HALF).astype(BF16)
        )
        if g == 0:
            pl.semaphore_wait(barrier, len(peers))
        for p in range(many * g, many * (g + 1)):

            def begin(k, carry, p=p):
                block(p, k, sub).start()
                return carry

            lax.fori_loop(1, across, begin, 0)
            own = rows(p * across + sub, BLK)
            returned[own, :] = results[own, :]

    def landed(p):
        def one(k, carry):
            block(p, k, lax.rem(sub + across - k, across)).wait_recv()
            return carry

        lax.fori_loop(1, across, one, 0)

    def weighed(dy, c):
        p = position(dy, ny)
        return dot(
            weigh_ref[(ny - dy) % ny],
            returned[p * group : (p + 1) * group, c * wide : (c + 1) * wide],
        )

    def to_right(step, c):
        sem = step * chunks + c
        return remote(
            right_out.at[step, c], right_in.at[step, c], right_send.at[sem], right_recv.at[sem], at_y(1)
        )

    def to_left(step, c):
        sem = step * chunks + c
        return remote(
            left_out.at[step, c], left_in.at[step, c], left_send.at[sem], left_recv.at[sem], at_y(ny - 1)
        )

    def advance(dy):
        landed(position(dy, ny))
        for c in range(chunks):
            right = way(dy, c, ny) == 1
            step = reach - dy if right else dy - reach
            begins = dy == reach or way(dy + 1 if right else dy - 1, c, ny) != way(dy, c, ny)
            to, outbox, inbox = (
                (to_right, right_out, right_in) if right else (to_left, left_out, left_in)
            )
            total = weighed(dy, c)
            if not begins:
                to(step - 1, c).wait_recv()
                total = total + inbox[step - 1, c].astype(F32)
            outbox[step, c] = total.astype(BF16)
            to(step, c).start()

    for g in range(ny // many):
        compute(g)
    for dy in sorted(range(1, ny), key=lambda dy: position(dy, ny)):
        advance(dy)
    landed(ny - 1)
    for c in range(chunks):
        total = weighed(0, c)
        to_right(reach - 1, c).wait_recv()
        to_left(reach - 1, c).wait_recv()
        total = total + right_in[reach - 1, c].astype(F32) + left_in[reach - 1, c].astype(F32)
        for half in range(2):
            cols = slice(half * HALF + c * wide, half * HALF + (c + 1) * wide)
            out_ref[:, cols] = (
                stream_ref[:, cols].astype(F32) + total[half * tokens : (half + 1) * tokens, :]
            ).astype(BF16)
    for c in range(chunks):
        for dy in range(1, ny):
            if way(dy, c, ny) == 1:
                to_right(reach - dy, c).wait_send()
            else:
                to_left(dy - reach, c).wait_send()
    for p in range(ny):

        def finish(k, carry, p=p):
            block(p, k, sub).wait_send()
            return carry

        lax.fori_loop(1, across, finish, 0)


def in_vmem(n):
    return [pl.BlockSpec(memory_space=pltpu.VMEM)] * n


def shards(
    nx, ny,
    query_proj, key_proj, value_proj, init_state, residual, out_gain, proj_weight, moe_gain,
    w_gate, w_up, w_down, expert_ids, gate_weights,
):
    tok, width = query_proj.shape[1:]
    heads = width // HD
    part = heads // nx
    token_rows = residual.shape[1]
    count = nx * ny * 2
    slots = count * BLK
    group = 2 * nx * BLK

    state = (part, HD, HD)
    nz = lax.axis_size("expert")
    depth, shard = proj_weight.shape
    dma = pltpu.SemaphoreType.DMA
    stream, weighing, incoming, *full = pl.pallas_call(
        functools.partial(front_kernel, nx, ny, nz),
        out_shape=[
            jax.ShapeDtypeStruct((token_rows, D), BF16),
            jax.ShapeDtypeStruct((ny, 2 * token_rows, group), BF16),
            jax.ShapeDtypeStruct((slots, HALF), BF16),
            *[jax.ShapeDtypeStruct((nz, *w_down.shape[1:]), BF16)] * 3,
        ],
        in_specs=[*in_vmem(10), *[pl.BlockSpec(memory_space=pl.ANY)] * 3],
        out_specs=[*in_vmem(2), *[pl.BlockSpec(memory_space=pl.ANY)] * 4],
        scratch_shapes=[
            pltpu.VMEM((nx, *state), BF16),
            pltpu.VMEM((nx, *state), BF16),
            pltpu.VMEM(state, BF16),
            pltpu.VMEM((ny, *state), BF16),
            pltpu.VMEM((nx, *state), BF16),
            pltpu.VMEM((nx, *state), BF16),
            pltpu.VMEM((tok, width), F32),
            pltpu.VMEM((tok, width), BF16),
            pltpu.VMEM((nz, nx, ny, depth // (nx * ny), shard), BF16),
            pltpu.VMEM((tok, D), F32),
            pltpu.VMEM((token_rows, D), BF16),
            pltpu.VMEM((token_rows, D), BF16),
            pltpu.VMEM((ny, 2 * token_rows, group), BF16),
            pltpu.VMEM((ny, 2 * token_rows, group), BF16),
            pltpu.VMEM((ny, CHUNKS, 2 * token_rows, HALF // CHUNKS), BF16),
            pltpu.VMEM((slots, HALF), BF16),
            *[dma((n,)) for n in (nx, nx, ny, ny, nx, nx, nz, nz, ny, ny, ny, ny, ny, ny, ny, ny, 2)],
            *[dma((n,)) for n in (ny, ny, ny, ny * CHUNKS, ny * CHUNKS, count, count)],
            *[dma((n,)) for n in (nx, nx, 2 * ny, 2 * ny, 6 * nz, 6 * nz, 3)],
        ],
        compiler_params=pltpu.CompilerParams(
            collective_id=0, has_side_effects=True, vmem_limit_bytes=VMEM_LIMIT
        ),
        cost_estimate=pl.CostEstimate(flops=10**9, bytes_accessed=3 * 10**8, transcendentals=0),
        name="front",
    )(
        query_proj[0], key_proj[0], value_proj[0], init_state[0], out_gain[None, :], proj_weight,
        residual[0], moe_gain[None, :], expert_ids.transpose(2, 0, 1), gate_weights.transpose(2, 0, 1), w_gate[0], w_up[0], w_down[0],
    )

    passing = (CHUNKS, 2 * token_rows, HALF // CHUNKS)
    out = pl.pallas_call(
        functools.partial(expert_kernel, nx, ny),
        out_shape=jax.ShapeDtypeStruct((token_rows, D), BF16),
        in_specs=in_vmem(6),
        out_specs=pl.BlockSpec(memory_space=pltpu.VMEM),
        scratch_shapes=[
            pltpu.VMEM((slots, HALF), BF16),
            pltpu.VMEM((slots, HALF), BF16),
            *[pltpu.VMEM((n, *passing), BF16) for n in [ny // 2] * 4],
            *[dma((n,)) for n in (count, count)],
            *[dma((n * CHUNKS,)) for n in [ny // 2] * 4],
        ],
        compiler_params=pltpu.CompilerParams(
            collective_id=2, has_side_effects=True, vmem_limit_bytes=VMEM_LIMIT
        ),
        cost_estimate=pl.CostEstimate(flops=5 * 10**9, bytes_accessed=2 * 10**8, transcendentals=0),
        name="experts",
    )(incoming, *full, stream, weighing)
    return out[None]


def solution(mesh):
    placed = (
        P("expert", "seq", "head"),
        P("expert", "seq", "head"),
        P("expert", "seq", "head"),
        P("expert", "head", None, None),
        P("expert", ("seq", "head"), None),
        P("head"),
        P("head", "expert"),
        P(),
        P(("seq", "head"), None, "expert"),
        P(("seq", "head"), None, "expert"),
        P(("seq", "head"), None, "expert"),
        P("expert", ("seq", "head"), None),
        P("expert", ("seq", "head"), None),
    )
    nx, ny = grid_of(mesh.shape["seq"])
    return jax.shard_map(
        functools.partial(shards, nx, ny),
        mesh=mesh,
        in_specs=placed,
        out_specs=P("expert", ("seq", "head"), None),
        check_vma=False,
    )
```

```python
import functools

import jax
import jax.numpy as jnp
from jax import lax
from jax.experimental import pallas as pl
from jax.experimental.pallas import tpu as pltpu
from jax.sharding import PartitionSpec as P

D = 2048
HALF = 1024
HD = 128
TOP = 6
CAP = 8
BLK = 2 * CAP
MESH = pl.DeviceIdType.MESH
BF16 = jnp.bfloat16
F32 = jnp.float32
CHUNKS = 2
VMEM_LIMIT = 56 * 2**20


def grid_of(seq):
    nx = 4 if seq == 32 else 2
    return nx, seq // nx


def dot(a, b, dims=((1,), (0,))):
    return lax.dot_general(a, b, (dims, ((), ())), preferred_element_type=F32)


def rows(index, size):
    return pl.ds(pl.multiple_of(index * size, size), size)


def remote(src, dst, send, recv, target):
    return pltpu.make_async_remote_copy(
        src_ref=src, dst_ref=dst, send_sem=send, recv_sem=recv, device_id=target, device_id_type=MESH
    )


def position(dy, ny):
    if dy == 0:
        return ny - 1
    return ny - 2 * dy if dy <= ny // 2 else 2 * dy - ny - 1


def way(b, c, n):
    return 1 if b < n // 2 or (b == n // 2 and c == 0) else n - 1


def onward(b, c, n):
    step = way(b, c, n)
    further = (b + step) % n
    return step if further and way(further, c, n) == step else None


def place(ids_ref, gates_ref, weighing):
    tokens = ids_ref.shape[2]
    groups, _, group = weighing.shape
    slots = groups * group
    experts = slots // BLK
    expert = lax.broadcasted_iota(jnp.int32, (experts, tokens), 0)
    chosen = jnp.zeros((experts, tokens), F32)
    gates = jnp.zeros((experts, tokens), F32)
    for k in range(TOP):
        match = ids_ref[k] == expert
        chosen = chosen + jnp.where(match, 1.0, 0.0)
        gates = gates + jnp.where(match, gates_ref[k], 0.0)
    earlier = lax.broadcasted_iota(jnp.int32, (tokens, tokens), 0) < lax.broadcasted_iota(
        jnp.int32, (tokens, tokens), 1
    )
    earlier = jnp.where(earlier, 1.0, 0.0).astype(BF16)
    order = dot(chosen.astype(BF16), earlier)
    turn = (chosen * (order + 1.0)).astype(BF16)
    spread = lax.broadcasted_iota(jnp.int32, (experts, slots), 1) // BLK == lax.broadcasted_iota(
        jnp.int32, (experts, slots), 0
    )
    spread = jnp.where(spread, 1.0, 0.0).astype(BF16)
    turn = dot(turn, spread, ((0,), (0,)))
    gates = dot(gates.astype(BF16), spread, ((0,), (0,)))
    slot = lax.broadcasted_iota(jnp.int32, (tokens, slots), 1)
    place_in = lax.rem(slot, BLK)
    for half in range(2):
        wanted = (place_in - (half * CAP - 1)).astype(F32)
        hit = (turn == wanted) & (place_in // CAP == half)
        weights = jnp.where(hit, gates, 0.0).astype(BF16)
        for i in range(groups):
            weighing[i, half * tokens : (half + 1) * tokens, :] = weights[:, i * group : (i + 1) * group]


def run_experts(
    nx, ny, x_ref, gate_ref, up_ref, down_ref, stream_ref, weigh_ref, out_ref, results, returned, right_out, right_in, left_out, left_in,
    send, recv, right_send, right_recv, left_send, left_recv,
):
    s, h, z = lax.axis_index("seq"), lax.axis_index("head"), lax.axis_index("expert")
    y, x = s // nx, lax.rem(s, nx)
    across = 2 * nx
    sub = x * 2 + h
    reach = ny // 2
    group = across * BLK
    tokens = stream_ref.shape[0]
    many = ny // 2
    shards_in_half = down_ref.shape[0] // 2
    chunks, wide = right_out.shape[1], right_out.shape[3]

    def at_sub(k):
        other = lax.rem(sub + k, across)
        return (y * nx + other // 2, lax.rem(other, 2), z)

    def at_y(d):
        return (lax.rem(y + d, ny) * nx + x, h, z)

    def block(p, k, source):
        slot = p * across + lax.rem(sub + k, across)
        sem = p * across + k
        return remote(
            results.at[rows(slot, BLK), :], returned.at[rows(p * across + source, BLK), :],
            send.at[sem], recv.at[sem], at_sub(k),
        )

    def compute(g):
        span = slice(many * g * group, many * (g + 1) * group)
        blocks = x_ref[span, :].astype(F32).reshape(many * across, BLK, HALF)
        low = blocks[:, :CAP].reshape(many * across * CAP, HALF).astype(BF16)
        high = blocks[:, CAP:].reshape(many * across * CAP, HALF).astype(BF16)
        acts = []
        for w_ref in (gate_ref, up_ref):
            total = None
            for i, values in enumerate((low, high)):
                for j in range(shards_in_half):
                    wide_in = HALF // shards_in_half
                    term = dot(
                        values[:, j * wide_in : (j + 1) * wide_in], w_ref[i * shards_in_half + j], ((1,), (1,))
                    )
                    total = term if total is None else total + term
            acts.append(total)
        gate, up = acts
        hidden = (gate / (1.0 + jnp.exp(-gate)) * up).astype(BF16)
        outs = [
            jnp.concatenate(
                [dot(hidden, down_ref[i * shards_in_half + j]) for j in range(shards_in_half)], axis=1
            ).reshape(many * across, CAP, HALF)
            for i in range(2)
        ]
        results[span, :] = (
            jnp.concatenate(outs, axis=1).reshape(many * across * BLK, HALF).astype(BF16)
        )
        for p in range(many * g, many * (g + 1)):

            def begin(k, carry, p=p):
                block(p, k, sub).start()
                return carry

            lax.fori_loop(1, across, begin, 0)
            own = rows(p * across + sub, BLK)
            returned[own, :] = results[own, :]

    def landed(p):
        def one(k, carry):
            block(p, k, lax.rem(sub + across - k, across)).wait_recv()
            return carry

        lax.fori_loop(1, across, one, 0)

    def weighed(dy, c):
        p = position(dy, ny)
        return dot(
            weigh_ref[(ny - dy) % ny],
            returned[p * group : (p + 1) * group, c * wide : (c + 1) * wide],
        )

    def to_right(step, c):
        sem = step * chunks + c
        return remote(
            right_out.at[step, c], right_in.at[step, c], right_send.at[sem], right_recv.at[sem], at_y(1)
        )

    def to_left(step, c):
        sem = step * chunks + c
        return remote(
            left_out.at[step, c], left_in.at[step, c], left_send.at[sem], left_recv.at[sem], at_y(ny - 1)
        )

    def advance(dy):
        landed(position(dy, ny))
        for c in range(chunks):
            right = way(dy, c, ny) == 1
            step = reach - dy if right else dy - reach
            begins = dy == reach or way(dy + 1 if right else dy - 1, c, ny) != way(dy, c, ny)
            to, outbox, inbox = (
                (to_right, right_out, right_in) if right else (to_left, left_out, left_in)
            )
            total = weighed(dy, c)
            if not begins:
                to(step - 1, c).wait_recv()
                total = total + inbox[step - 1, c].astype(F32)
            outbox[step, c] = total.astype(BF16)
            to(step, c).start()

    for g in range(ny // many):
        compute(g)
    for dy in sorted(range(1, ny), key=lambda dy: position(dy, ny)):
        advance(dy)
    landed(ny - 1)
    for c in range(chunks):
        total = weighed(0, c)
        to_right(reach - 1, c).wait_recv()
        to_left(reach - 1, c).wait_recv()
        total = total + right_in[reach - 1, c].astype(F32) + left_in[reach - 1, c].astype(F32)
        for half in range(2):
            cols = slice(half * HALF + c * wide, half * HALF + (c + 1) * wide)
            out_ref[:, cols] = (
                stream_ref[:, cols].astype(F32) + total[half * tokens : (half + 1) * tokens, :]
            ).astype(BF16)
    for c in range(chunks):
        for dy in range(1, ny):
            if way(dy, c, ny) == 1:
                to_right(reach - dy, c).wait_send()
            else:
                to_left(dy - reach, c).wait_send()
    for p in range(ny):

        def finish(k, carry, p=p):
            block(p, k, sub).wait_send()
            return carry

        lax.fori_loop(1, across, finish, 0)


def layer_kernel(
    nx, ny, nz, q_ref, k_ref, v_ref, init_ref, out_gain_ref, wo_ref, res_ref, gain_ref, ids_ref, gates_ref, gate_ref, up_ref, down_ref,
    out_ref,
    stream_ref, incoming_ref, gate_full_ref, up_full_ref, down_full_ref,
    loc, xin, tot, yin, pre, pin, att, mixed, wo, proj, snd, rcv, own_weighing, weighing, feats, outgoing,
    x_send, x_recv, y_send, y_recv, p_send, p_recv, wz_send, wz_recv, wy_send, wy_recv,
    right_send, right_recv, left_send, left_recv, pass_send, pass_recv, h_sem, g_send, g_recv, own_sem,
    f_send, f_recv, send, recv, bx_send, bx_recv, by_send, by_recv, ring_send, ring_recv, ring_own,
    *for_experts,
):
    s, h, z = lax.axis_index("seq"), lax.axis_index("head"), lax.axis_index("expert")
    y, x = s // nx, lax.rem(s, nx)
    across = 2 * nx
    sub = x * 2 + h
    heads = q_ref.shape[1] // HD
    part = heads // nx
    tokens = res_ref.shape[0]
    depth, width = wo.shape[3:]
    reach = ny // 2
    cross = 6 * nz // 8

    def at_sub(k):
        other = lax.rem(sub + k, across)
        return (y * nx + other // 2, lax.rem(other, 2), z)

    def at_x(d):
        return (y * nx + lax.rem(x + d, nx), h, z)

    def at_y(d):
        return (lax.rem(y + d, ny) * nx + x, h, z)

    def at_z(d):
        return (s, h, lax.rem(z + d, nz))

    barrier = pltpu.get_barrier_semaphore()
    peers = [at_z(d) for d in range(1, nz)]
    peers += [at_y(d) for d in range(1, ny)]
    peers += [at_sub(d) for d in range(1, across)]
    for peer in peers:
        pl.semaphore_signal(barrier, inc=1, device_id=peer, device_id_type=MESH)
    with jax.named_scope("states"):
        for i in range(heads):
            cols = slice(i * HD, (i + 1) * HD)
            loc[i // part, i % part] = dot(k_ref[:, cols], v_ref[:, cols], ((0,), (0,))).astype(BF16)
    with jax.named_scope("barrier"):
        pl.semaphore_wait(barrier, len(peers))

    first = [
        remote(loc.at[lax.rem(x + d, nx)], xin.at[d], x_send.at[d], x_recv.at[d], at_x(d))
        for d in range(1, nx)
    ]
    for copy in first:
        copy.start()

    shares = (gate_ref, up_ref, down_ref)
    fulls = (gate_full_ref, up_full_ref, down_full_ref)
    pieces = 2 * len(shares)
    half_rows = gate_ref.shape[0] // 2

    def piece(b, i, step):
        span = pl.ds(i % 2 * half_rows, half_rows)
        there = fulls[i // 2].at[lax.rem(z + nz - b, nz), span, :]
        sem = (b + step) % nz * pieces + i
        return remote(
            there if b else shares[i // 2].at[span, :], there, ring_send.at[sem], ring_recv.at[sem], at_z(step)
        )

    def piece_came(b, i):
        span = pl.ds(i % 2 * half_rows, half_rows)
        there = fulls[i // 2].at[lax.rem(z + nz - b, nz), span, :]
        sem = b * pieces + i
        return remote(there, there, ring_send.at[sem], ring_recv.at[sem], at_z(1))

    def relay_ring(distance, later):
        for i in range(later * pieces // 2, (later + 1) * pieces // 2):
            for b in sorted({distance, nz - distance}):
                piece_came(b, i).wait_recv()
                step = onward(b, later, nz)
                if step:
                    piece(b, i, step).start()

    mine = rows(x * ny + y, depth)

    def fetch(d, owner):
        return remote(
            wo_ref.at[mine, :], wo.at[owner, x, y], wz_send.at[d], wz_recv.at[d], at_z(d)
        )

    for d in range(1, nz):
        fetch(d, z).start()
    for i in range(pieces):
        for step in (1, nz - 1):
            piece(0, i, step).start()
    kept = [
        pltpu.make_async_copy(share, full.at[z], ring_own.at[i])
        for i, (share, full) in enumerate(zip(shares, fulls, strict=True))
    ]
    for copy in kept:
        copy.start()

    def chip(dx, b):
        return wo.at[pl.ds(0, cross), lax.rem(x + dx, nx), lax.rem(y + ny - b, ny)]

    def along_y(b, step):
        arrives = (b + step) % ny
        return remote(chip(0, b), chip(0, b), wy_send.at[arrives], wy_recv.at[arrives], at_y(step))

    def landed_y(b):
        return remote(chip(0, b), chip(0, b), wy_send.at[b], wy_recv.at[b], at_y(1))

    def along_x(b, dx, sends, recvs, step):
        return remote(chip(dx, b), chip(dx, b), sends.at[b], recvs.at[b], at_x(step))

    rest = pl.ds(cross, nz - cross)

    def side(d):
        own = wo.at[rest, x, y]
        return remote(own, own, bx_send.at[d], bx_recv.at[d], at_x(d))

    def side_came(d):
        there = wo.at[rest, lax.rem(x + nx - d, nx), y]
        return remote(there, there, bx_send.at[d], bx_recv.at[d], at_x(d))

    def row(b, c, step):
        part_of = wo.at[rest, pl.ds(c * (nx // 2), nx // 2), lax.rem(y + ny - b, ny)]
        sem = (b + step) % ny * 2 + c
        return remote(part_of, part_of, by_send.at[sem], by_recv.at[sem], at_y(step))

    def row_came(b, c):
        there = wo.at[rest, pl.ds(c * (nx // 2), nx // 2), lax.rem(y + ny - b, ny)]
        sem = b * 2 + c
        return remote(there, there, by_send.at[sem], by_recv.at[sem], at_y(1))

    def relay_row(b):
        for c in range(2):
            row_came(b, c).wait_recv()
            step = onward(b, c, ny)
            if step:
                row(b, c, step).start()

    to_right = [0, *range(reach + 1, ny)]

    def spread(b):
        along_x(b, 0, right_send, right_recv, 1).start()
        along_x(b, 0, left_send, left_recv, nx - 1).start()

    def relay_y(b):
        landed_y(b).wait_recv()
        if b < reach:
            along_y(b, 1).start()
        elif b > reach + 1:
            along_y(b, ny - 1).start()
        spread(b)

    def relay_x(b):
        if b in to_right:
            along_x(b, nx - 1, right_send, right_recv, 1).wait_recv()
            along_x(b, nx - 1, pass_send, pass_recv, 1).start()
        else:
            along_x(b, 1, left_send, left_recv, nx - 1).wait_recv()
            along_x(b, 1, pass_send, pass_recv, nx - 1).start()

    with jax.named_scope("states_x"):
        xin[0] = loc[x]
        for copy in first:
            copy.wait_recv()
    tot[...] = sum(xin[d].astype(F32) for d in range(nx)).astype(BF16)
    second = [remote(tot, yin.at[d], y_send.at[d], y_recv.at[d], at_y(d)) for d in range(1, ny)]
    for copy in second:
        copy.start()

    with jax.named_scope("fetched"):
        wo[z, x, y] = wo_ref[mine, :]
        for d in range(1, nz):
            fetch(d, lax.rem(z + nz - d, nz)).wait_recv()
    along_y(0, 1).start()
    along_y(0, ny - 1).start()
    for d in range(1, nx):
        side(d).start()
    spread(0)

    with jax.named_scope("inner"):
        positions = q_ref.shape[0]
        causal = lax.broadcasted_iota(jnp.int32, (positions, positions), 0) >= lax.broadcasted_iota(
            jnp.int32, (positions, positions), 1
        )
        for i in range(heads):
            cols = slice(i * HD, (i + 1) * HD)
            scores = dot(q_ref[:, cols], k_ref[:, cols], ((1,), (1,)))
            scores = jnp.where(causal, scores, 0.0).astype(BF16)
            att[:, cols] = dot(scores, v_ref[:, cols])
    with jax.named_scope("placing"):
        place(ids_ref, gates_ref, own_weighing)
    with jax.named_scope("relay_1"):
        for d in range(1, nx):
            side_came(d).wait_recv()
        for c in range(2):
            for step in (1, ny - 1):
                row(0, c, step).start()
        relay_y(1)
        relay_y(ny - 1)
        relay_x(0)
        relay_row(1)
        relay_row(ny - 1)
        relay_ring(1, 0)

    before = jnp.zeros(tot.shape, F32)
    with jax.named_scope("states_y"):
        for d in range(1, ny):
            second[d - 1].wait_recv()
            before = before + yin[d].astype(F32) * (d <= y).astype(F32)
    third = []
    for e in range(nx):
        target = lax.rem(x + e, nx)
        state = before
        for d in range(nx):
            source = lax.rem(x + nx - d, nx)
            state = state + xin[d].astype(F32) * (source < target).astype(F32)
        pre[e] = state.astype(BF16)
        if e:
            copy = remote(pre.at[e], pin.at[e], p_send.at[e], p_recv.at[e], at_x(e))
            copy.start()
            third.append(copy)
    pin[0] = pre[0]
    with jax.named_scope("relay_2"):
        for step in range(2, reach):
            relay_y(step)
            relay_y(ny - step)
            relay_row(step)
            relay_row(ny - step)
            relay_x(step - 1)
            relay_x(ny - step + 1)
        relay_y(reach)
        relay_row(reach)
        relay_x(reach - 1)
        relay_x(reach + 1)
        relay_ring(1, 1)
    weighing[0] = own_weighing[y]
    shared = [
        remote(
            own_weighing.at[lax.rem(y + d, ny)], weighing.at[d], g_send.at[d], g_recv.at[d], at_y(d)
        )
        for d in range(1, ny)
    ]
    for copy in shared:
        copy.start()
    with jax.named_scope("mix"):
        for e in range(nx):
            if e:
                third[e - 1].wait_recv()
            for j in range(part):
                head = lax.rem(x + nx - e, nx) * part + j
                cols = rows(head, HD)
                state = (init_ref[head] + pin[e, j].astype(F32)).astype(BF16)
                out = att[:, cols] + dot(q_ref[:, cols], state)
                inv = lax.rsqrt(jnp.mean(out * out, axis=1, keepdims=True) + 1e-05)
                mixed[:, cols] = (out * inv * out_gain_ref[:, cols]).astype(BF16)
    with jax.named_scope("relay_3"):
        relay_x(reach)
        for b in range(ny):
            if b in to_right:
                along_x(b, 1, left_send, left_recv, nx - 1).wait_recv()
                along_x(b, 2, pass_send, pass_recv, 1).wait_recv()
            else:
                along_x(b, nx - 1, right_send, right_recv, 1).wait_recv()
                along_x(b, 2, pass_send, pass_recv, nx - 1).wait_recv()

    relay_ring(2, 0)
    with jax.named_scope("project"):
        for c in range(nz):
            proj[:, c * width : (c + 1) * width] = dot(mixed[...], wo[c].reshape(nx * ny * depth, width))
    snd[...] = proj[rows(1 - h, tokens), :].astype(BF16)
    half = remote(snd, rcv, h_sem.at[0], h_sem.at[1], (s, 1 - h, z))
    half.start()
    relay_ring(2, 1)
    for copy in first + second + third:
        copy.wait_send()
    for d in range(1, nz):
        fetch(d, z).wait_send()
    for b in range(ny):
        along_x(b, 0, right_send, right_recv, 1).wait_send()
        along_x(b, 0, left_send, left_recv, nx - 1).wait_send()
        if b in to_right:
            along_x(b, nx - 1, pass_send, pass_recv, 1).wait_send()
        else:
            along_x(b, 1, pass_send, pass_recv, nx - 1).wait_send()
        if b and b <= reach:
            along_y(b - 1, 1).wait_send()
        elif b:
            along_y((b + 1) % ny, ny - 1).wait_send()
        if b:
            for c in range(2):
                row_came(b, c).wait_send()
    for d in range(1, nx):
        side(d).wait_send()
    with jax.named_scope("other_half"):
        half.wait_recv()
    stream = (
        res_ref[...].astype(F32) + (proj[rows(h, tokens), :] + rcv[...].astype(F32))
    ).astype(BF16)
    stream_ref[...] = stream
    stream_f = stream.astype(F32)
    inv = lax.rsqrt(jnp.mean(stream_f * stream_f, axis=1, keepdims=True) + 1e-06)
    moe_in = (stream_f * inv * gain_ref[...]).astype(BF16)
    chunks, wide = feats.shape[1], feats.shape[3]
    for c in range(chunks):
        feats[0, c, :tokens, :] = moe_in[:, c * wide : (c + 1) * wide]
        feats[0, c, tokens:, :] = moe_in[:, HALF + c * wide : HALF + (c + 1) * wide]

    def ring(b, c, step):
        arrives = (b + step) % ny
        sem = arrives * chunks + c
        return remote(
            feats.at[b, c], feats.at[arrives, c], f_send.at[sem], f_recv.at[sem], at_y(step)
        )

    for c in range(chunks):
        ring(0, c, 1).start()
        ring(0, c, ny - 1).start()
    for d in range(1, ny):
        shared[d - 1].wait_recv()

    def block(b, k):
        other = lax.rem(sub + k, across)
        slot = position((ny - b) % ny, ny) * across + sub
        sem = b * across + k
        return remote(
            outgoing.at[rows(b * across + other, BLK), :], incoming_ref.at[rows(slot, BLK), :],
            send.at[sem], recv.at[sem], at_sub(k),
        )

    def arrived(b, k):
        other = lax.rem(sub + across - k, across)
        slot = position((ny - b) % ny, ny) * across + other
        sem = b * across + k
        return remote(
            outgoing.at[rows(b * across + other, BLK), :], incoming_ref.at[rows(slot, BLK), :],
            send.at[sem], recv.at[sem], at_sub(k),
        )

    def keep(b):
        slot = position((ny - b) % ny, ny) * across + sub
        return pltpu.make_async_copy(
            outgoing.at[rows(b * across + sub, BLK), :], incoming_ref.at[rows(slot, BLK), :], own_sem.at[b]
        )

    group = across * BLK
    around = [0]
    for step in range(1, reach):
        around += [step, ny - step]
    around.append(reach)
    for b in around:
        if b == 2:
            relay_ring(3, 0)
        if b == reach:
            relay_ring(3, 1)
        picks = jnp.where(weighing[b].astype(F32) > 0.0, 1.0, 0.0).astype(BF16)
        for c in range(chunks):
            if b:
                step = way(b, c, ny)
                ring((b - step) % ny, c, step).wait_recv()
                step = onward(b, c, ny)
                if step:
                    ring(b, c, step).start()
            outgoing[b * group : (b + 1) * group, c * wide : (c + 1) * wide] = dot(
                picks, feats[b, c], ((0,), (0,))
            ).astype(BF16)

        def begin(k, carry, b=b):
            block(b, k).start()
            return carry

        lax.fori_loop(1, across, begin, 0)
        keep(b).start()

    half.wait_send()
    for copy in shared:
        copy.wait_send()
    for b in range(1, ny):
        for c in range(chunks):
            step = way(b, c, ny)
            ring((b - step) % ny, c, step).wait_send()
    for later in range(2):
        relay_ring(nz // 2, later)
    for copy in kept:
        copy.wait()
    for b in range(1, nz):
        for i in range(pieces):
            piece_came(b, i).wait_send()
    for b in around:
        keep(b).wait()

        def finish(k, carry, b=b):
            block(b, k).wait_send()
            arrived(b, k).wait_recv()
            return carry

        lax.fori_loop(1, across, finish, 0)

    run_experts(
        nx, ny, incoming_ref, gate_full_ref, up_full_ref, down_full_ref, stream_ref, weighing, out_ref, *for_experts
    )


def in_vmem(n):
    return [pl.BlockSpec(memory_space=pltpu.VMEM)] * n


def shards(
    nx, ny,
    query_proj, key_proj, value_proj, init_state, residual, out_gain, proj_weight, moe_gain,
    w_gate, w_up, w_down, expert_ids, gate_weights,
):
    tok, width = query_proj.shape[1:]
    heads = width // HD
    part = heads // nx
    token_rows = residual.shape[1]
    count = nx * ny * 2
    slots = count * BLK
    group = 2 * nx * BLK

    state = (part, HD, HD)
    nz = lax.axis_size("expert")
    depth, shard = proj_weight.shape
    dma = pltpu.SemaphoreType.DMA
    passing = (CHUNKS, 2 * token_rows, HALF // CHUNKS)
    out = pl.pallas_call(
        functools.partial(layer_kernel, nx, ny, nz),
        out_shape=jax.ShapeDtypeStruct((token_rows, D), BF16),
        in_specs=[*in_vmem(10), *[pl.BlockSpec(memory_space=pl.ANY)] * 3],
        out_specs=pl.BlockSpec(memory_space=pltpu.VMEM),
        scratch_shapes=[
            pltpu.VMEM((token_rows, D), BF16),
            pltpu.VMEM((slots, HALF), BF16),
            *[pltpu.VMEM((nz, *w_down.shape[1:]), BF16)] * 3,
            pltpu.VMEM((nx, *state), BF16),
            pltpu.VMEM((nx, *state), BF16),
            pltpu.VMEM(state, BF16),
            pltpu.VMEM((ny, *state), BF16),
            pltpu.VMEM((nx, *state), BF16),
            pltpu.VMEM((nx, *state), BF16),
            pltpu.VMEM((tok, width), F32),
            pltpu.VMEM((tok, width), BF16),
            pltpu.VMEM((nz, nx, ny, depth // (nx * ny), shard), BF16),
            pltpu.VMEM((tok, D), F32),
            pltpu.VMEM((token_rows, D), BF16),
            pltpu.VMEM((token_rows, D), BF16),
            pltpu.VMEM((ny, 2 * token_rows, group), BF16),
            pltpu.VMEM((ny, 2 * token_rows, group), BF16),
            pltpu.VMEM((ny, CHUNKS, 2 * token_rows, HALF // CHUNKS), BF16),
            pltpu.VMEM((slots, HALF), BF16),
            *[dma((n,)) for n in (nx, nx, ny, ny, nx, nx, nz, nz, ny, ny, ny, ny, ny, ny, ny, ny, 2)],
            *[dma((n,)) for n in (ny, ny, ny, ny * CHUNKS, ny * CHUNKS, count, count)],
            *[dma((n,)) for n in (nx, nx, 2 * ny, 2 * ny, 6 * nz, 6 * nz, 3)],
            pltpu.VMEM((slots, HALF), BF16),
            pltpu.VMEM((slots, HALF), BF16),
            *[pltpu.VMEM((n, *passing), BF16) for n in [ny // 2] * 4],
            *[dma((n,)) for n in (count, count)],
            *[dma((n * CHUNKS,)) for n in [ny // 2] * 4],
        ],
        compiler_params=pltpu.CompilerParams(
            collective_id=0, has_side_effects=True, vmem_limit_bytes=VMEM_LIMIT
        ),
        cost_estimate=pl.CostEstimate(flops=10**9, bytes_accessed=3 * 10**8, transcendentals=0),
        name="layer",
    )(
        query_proj[0], key_proj[0], value_proj[0], init_state[0], out_gain[None, :], proj_weight,
        residual[0], moe_gain[None, :], expert_ids.transpose(2, 0, 1), gate_weights.transpose(2, 0, 1), w_gate[0], w_up[0], w_down[0],
    )
    return out[None]


def solution(mesh):
    placed = (
        P("expert", "seq", "head"),
        P("expert", "seq", "head"),
        P("expert", "seq", "head"),
        P("expert", "head", None, None),
        P("expert", ("seq", "head"), None),
        P("head"),
        P("head", "expert"),
        P(),
        P(("seq", "head"), None, "expert"),
        P(("seq", "head"), None, "expert"),
        P(("seq", "head"), None, "expert"),
        P("expert", ("seq", "head"), None),
        P("expert", ("seq", "head"), None),
    )
    nx, ny = grid_of(mesh.shape["seq"])
    return jax.shard_map(
        functools.partial(shards, nx, ny),
        mesh=mesh,
        in_specs=placed,
        out_specs=P("expert", ("seq", "head"), None),
        check_vma=False,
    )
```

```python
import functools

import jax
import jax.numpy as jnp
from jax import lax
from jax.experimental import pallas as pl
from jax.experimental.pallas import tpu as pltpu
from jax.sharding import PartitionSpec as P

D = 2048
HALF = 1024
HD = 128
TOP = 6
CAP = 8
BLK = 2 * CAP
MESH = pl.DeviceIdType.MESH
BF16 = jnp.bfloat16
F32 = jnp.float32
CHUNKS = 2
VMEM_LIMIT = 56 * 2**20


def grid_of(seq):
    nx = 4 if seq == 32 else 2
    return nx, seq // nx


def dot(a, b, dims=((1,), (0,))):
    return lax.dot_general(a, b, (dims, ((), ())), preferred_element_type=F32)


def rows(index, size):
    return pl.ds(pl.multiple_of(index * size, size), size)


def remote(src, dst, send, recv, target):
    return pltpu.make_async_remote_copy(
        src_ref=src, dst_ref=dst, send_sem=send, recv_sem=recv, device_id=target, device_id_type=MESH
    )


def position(dy, ny):
    if dy == 0:
        return ny - 1
    return ny - 2 * dy if dy <= ny // 2 else 2 * dy - ny - 1


def way(b, c, n):
    return 1 if b < n // 2 or (b == n // 2 and c == 0) else n - 1


def onward(b, c, n):
    step = way(b, c, n)
    further = (b + step) % n
    return step if further and way(further, c, n) == step else None


def place(ids_ref, gates_ref, weighing):
    tokens = ids_ref.shape[2]
    groups, _, group = weighing.shape
    slots = groups * group
    experts = slots // BLK
    expert = lax.broadcasted_iota(jnp.int32, (experts, tokens), 0)
    chosen = jnp.zeros((experts, tokens), F32)
    gates = jnp.zeros((experts, tokens), F32)
    for k in range(TOP):
        match = ids_ref[k] == expert
        chosen = chosen + jnp.where(match, 1.0, 0.0)
        gates = gates + jnp.where(match, gates_ref[k], 0.0)
    earlier = lax.broadcasted_iota(jnp.int32, (tokens, tokens), 0) < lax.broadcasted_iota(
        jnp.int32, (tokens, tokens), 1
    )
    earlier = jnp.where(earlier, 1.0, 0.0).astype(BF16)
    order = dot(chosen.astype(BF16), earlier)
    turn = (chosen * (order + 1.0)).astype(BF16)
    spread = lax.broadcasted_iota(jnp.int32, (experts, slots), 1) // BLK == lax.broadcasted_iota(
        jnp.int32, (experts, slots), 0
    )
    spread = jnp.where(spread, 1.0, 0.0).astype(BF16)
    turn = dot(turn, spread, ((0,), (0,)))
    gates = dot(gates.astype(BF16), spread, ((0,), (0,)))
    slot = lax.broadcasted_iota(jnp.int32, (tokens, slots), 1)
    place_in = lax.rem(slot, BLK)
    for half in range(2):
        wanted = (place_in - (half * CAP - 1)).astype(F32)
        hit = (turn == wanted) & (place_in // CAP == half)
        weights = jnp.where(hit, gates, 0.0).astype(BF16)
        for i in range(groups):
            weighing[i, half * tokens : (half + 1) * tokens, :] = weights[:, i * group : (i + 1) * group]


def run_experts(
    nx, ny, nz, last, x_ref, gate_ref, up_ref, down_ref, stream_ref, weigh_ref, out_ref, results, returned, right_out, right_in, left_out, left_in,
    send, recv, right_send, right_recv, left_send, left_recv, spread_in, acts,
):
    s, h, z = lax.axis_index("seq"), lax.axis_index("head"), lax.axis_index("expert")
    y, x = s // nx, lax.rem(s, nx)
    across = 2 * nx
    sub = x * 2 + h
    reach = ny // 2
    group = across * BLK
    tokens = stream_ref.shape[0]
    many = ny // 2
    shards_in_half = down_ref.shape[0] // 2
    chunks, wide = right_out.shape[1], right_out.shape[3]

    def at_sub(k):
        other = lax.rem(sub + k, across)
        return (y * nx + other // 2, lax.rem(other, 2), z)

    def at_y(d):
        return (lax.rem(y + d, ny) * nx + x, h, z)

    def block(p, k, source):
        slot = p * across + lax.rem(sub + k, across)
        sem = p * across + k
        return remote(
            results.at[rows(slot, BLK), :], returned.at[rows(p * across + source, BLK), :],
            send.at[sem], recv.at[sem], at_sub(k),
        )

    group_rows = many * across * CAP

    def partial(g):
        span = slice(many * g * group, many * (g + 1) * group)
        mine = slice(g * group_rows, (g + 1) * group_rows)
        blocks = x_ref[span, :].astype(F32).reshape(many * across, BLK, HALF)
        wide_in = HALF // shards_in_half
        for i in range(2):
            values = blocks[:, i * CAP : (i + 1) * CAP].reshape(group_rows, HALF).astype(BF16)
            for j in range(shards_in_half):
                spread_in[i * shards_in_half + j, mine, :] = values[:, j * wide_in : (j + 1) * wide_in]
        for m, w_ref in enumerate((gate_ref, up_ref)):
            total = None
            for b in range(nz):
                if b == nz // 2:
                    continue
                owner = lax.rem(z + nz - b, nz)
                term = dot(spread_in[owner, mine, :], w_ref[owner], ((1,), (1,)))
                total = term if total is None else total + term
            acts[m, mine, :] = total

    def compute(g):
        span = slice(many * g * group, many * (g + 1) * group)
        mine = slice(g * group_rows, (g + 1) * group_rows)
        owner = lax.rem(z + nz // 2, nz)
        gate, up = (
            acts[m, mine, :] + dot(spread_in[owner, mine, :], w_ref[owner], ((1,), (1,)))
            for m, w_ref in enumerate((gate_ref, up_ref))
        )
        hidden = (gate / (1.0 + jnp.exp(-gate)) * up).astype(BF16)
        outs = [
            jnp.concatenate(
                [dot(hidden, down_ref[i * shards_in_half + j]) for j in range(shards_in_half)], axis=1
            ).reshape(many * across, CAP, HALF)
            for i in range(2)
        ]
        results[span, :] = (
            jnp.concatenate(outs, axis=1).reshape(many * across * BLK, HALF).astype(BF16)
        )
        for p in range(many * g, many * (g + 1)):

            def begin(k, carry, p=p):
                block(p, k, sub).start()
                return carry

            lax.fori_loop(1, across, begin, 0)
            own = rows(p * across + sub, BLK)
            returned[own, :] = results[own, :]

    def landed(p):
        def one(k, carry):
            block(p, k, lax.rem(sub + across - k, across)).wait_recv()
            return carry

        lax.fori_loop(1, across, one, 0)

    def weighed(dy, c):
        p = position(dy, ny)
        return dot(
            weigh_ref[(ny - dy) % ny],
            returned[p * group : (p + 1) * group, c * wide : (c + 1) * wide],
        )

    def to_right(step, c):
        sem = step * chunks + c
        return remote(
            right_out.at[step, c], right_in.at[step, c], right_send.at[sem], right_recv.at[sem], at_y(1)
        )

    def to_left(step, c):
        sem = step * chunks + c
        return remote(
            left_out.at[step, c], left_in.at[step, c], left_send.at[sem], left_recv.at[sem], at_y(ny - 1)
        )

    def advance(dy):
        landed(position(dy, ny))
        for c in range(chunks):
            right = way(dy, c, ny) == 1
            step = reach - dy if right else dy - reach
            begins = dy == reach or way(dy + 1 if right else dy - 1, c, ny) != way(dy, c, ny)
            to, outbox, inbox = (
                (to_right, right_out, right_in) if right else (to_left, left_out, left_in)
            )
            total = weighed(dy, c)
            if not begins:
                to(step - 1, c).wait_recv()
                total = total + inbox[step - 1, c].astype(F32)
            outbox[step, c] = total.astype(BF16)
            to(step, c).start()

    for g in range(ny // many):
        partial(g)
    last()
    for g in range(ny // many):
        compute(g)
    for dy in sorted(range(1, ny), key=lambda dy: position(dy, ny)):
        advance(dy)
    landed(ny - 1)
    for c in range(chunks):
        total = weighed(0, c)
        to_right(reach - 1, c).wait_recv()
        to_left(reach - 1, c).wait_recv()
        total = total + right_in[reach - 1, c].astype(F32) + left_in[reach - 1, c].astype(F32)
        for half in range(2):
            cols = slice(half * HALF + c * wide, half * HALF + (c + 1) * wide)
            out_ref[:, cols] = (
                stream_ref[:, cols].astype(F32) + total[half * tokens : (half + 1) * tokens, :]
            ).astype(BF16)
    for c in range(chunks):
        for dy in range(1, ny):
            if way(dy, c, ny) == 1:
                to_right(reach - dy, c).wait_send()
            else:
                to_left(dy - reach, c).wait_send()
    for p in range(ny):

        def finish(k, carry, p=p):
            block(p, k, sub).wait_send()
            return carry

        lax.fori_loop(1, across, finish, 0)


def layer_kernel(
    nx, ny, nz, q_ref, k_ref, v_ref, init_ref, out_gain_ref, wo_ref, res_ref, gain_ref, ids_ref, gates_ref, gate_ref, up_ref, down_ref,
    out_ref,
    stream_ref, incoming_ref, gate_full_ref, up_full_ref, down_full_ref,
    loc, xin, tot, yin, pre, pin, att, mixed, wo, proj, snd, rcv, own_weighing, weighing, feats, outgoing,
    x_send, x_recv, y_send, y_recv, p_send, p_recv, wz_send, wz_recv, wy_send, wy_recv,
    right_send, right_recv, left_send, left_recv, pass_send, pass_recv, h_sem, g_send, g_recv, own_sem,
    f_send, f_recv, send, recv, bx_send, bx_recv, by_send, by_recv, ring_send, ring_recv, ring_own,
    *for_experts,
):
    s, h, z = lax.axis_index("seq"), lax.axis_index("head"), lax.axis_index("expert")
    y, x = s // nx, lax.rem(s, nx)
    across = 2 * nx
    sub = x * 2 + h
    heads = q_ref.shape[1] // HD
    part = heads // nx
    tokens = res_ref.shape[0]
    depth, width = wo.shape[3:]
    reach = ny // 2
    cross = 6 * nz // 8

    def at_sub(k):
        other = lax.rem(sub + k, across)
        return (y * nx + other // 2, lax.rem(other, 2), z)

    def at_x(d):
        return (y * nx + lax.rem(x + d, nx), h, z)

    def at_y(d):
        return (lax.rem(y + d, ny) * nx + x, h, z)

    def at_z(d):
        return (s, h, lax.rem(z + d, nz))

    barrier = pltpu.get_barrier_semaphore()
    peers = [at_z(d) for d in range(1, nz)]
    peers += [at_y(d) for d in range(1, ny)]
    peers += [at_sub(d) for d in range(1, across)]
    for peer in peers:
        pl.semaphore_signal(barrier, inc=1, device_id=peer, device_id_type=MESH)
    with jax.named_scope("states"):
        for i in range(heads):
            cols = slice(i * HD, (i + 1) * HD)
            loc[i // part, i % part] = dot(k_ref[:, cols], v_ref[:, cols], ((0,), (0,))).astype(BF16)
    with jax.named_scope("barrier"):
        pl.semaphore_wait(barrier, len(peers))

    first = [
        remote(loc.at[lax.rem(x + d, nx)], xin.at[d], x_send.at[d], x_recv.at[d], at_x(d))
        for d in range(1, nx)
    ]
    for copy in first:
        copy.start()

    shares = (gate_ref, up_ref, down_ref)
    fulls = (gate_full_ref, up_full_ref, down_full_ref)
    pieces = 2 * len(shares)
    half_rows = gate_ref.shape[0] // 2

    def piece(b, i, step):
        span = pl.ds(i % 2 * half_rows, half_rows)
        there = fulls[i // 2].at[lax.rem(z + nz - b, nz), span, :]
        sem = (b + step) % nz * pieces + i
        return remote(
            there if b else shares[i // 2].at[span, :], there, ring_send.at[sem], ring_recv.at[sem], at_z(step)
        )

    def piece_came(b, i):
        span = pl.ds(i % 2 * half_rows, half_rows)
        there = fulls[i // 2].at[lax.rem(z + nz - b, nz), span, :]
        sem = b * pieces + i
        return remote(there, there, ring_send.at[sem], ring_recv.at[sem], at_z(1))

    def relay_ring(distance, later):
        for i in range(later * pieces // 2, (later + 1) * pieces // 2):
            for b in sorted({distance, nz - distance}):
                piece_came(b, i).wait_recv()
                step = onward(b, later, nz)
                if step:
                    piece(b, i, step).start()

    mine = rows(x * ny + y, depth)

    def fetch(d, owner):
        return remote(
            wo_ref.at[mine, :], wo.at[owner, x, y], wz_send.at[d], wz_recv.at[d], at_z(d)
        )

    for d in range(1, nz):
        fetch(d, z).start()
    for step in (1, nz - 1):
        piece(0, 0, step).start()
    kept = [
        pltpu.make_async_copy(share, full.at[z], ring_own.at[i])
        for i, (share, full) in enumerate(zip(shares, fulls, strict=True))
    ]
    for copy in kept:
        copy.start()

    def chip(dx, b):
        return wo.at[pl.ds(0, cross), lax.rem(x + dx, nx), lax.rem(y + ny - b, ny)]

    def along_y(b, step):
        arrives = (b + step) % ny
        return remote(chip(0, b), chip(0, b), wy_send.at[arrives], wy_recv.at[arrives], at_y(step))

    def landed_y(b):
        return remote(chip(0, b), chip(0, b), wy_send.at[b], wy_recv.at[b], at_y(1))

    def along_x(b, dx, sends, recvs, step):
        return remote(chip(dx, b), chip(dx, b), sends.at[b], recvs.at[b], at_x(step))

    rest = pl.ds(cross, nz - cross)

    def side(d):
        own = wo.at[rest, x, y]
        return remote(own, own, bx_send.at[d], bx_recv.at[d], at_x(d))

    def side_came(d):
        there = wo.at[rest, lax.rem(x + nx - d, nx), y]
        return remote(there, there, bx_send.at[d], bx_recv.at[d], at_x(d))

    def row(b, c, step):
        part_of = wo.at[rest, pl.ds(c * (nx // 2), nx // 2), lax.rem(y + ny - b, ny)]
        sem = (b + step) % ny * 2 + c
        return remote(part_of, part_of, by_send.at[sem], by_recv.at[sem], at_y(step))

    def row_came(b, c):
        there = wo.at[rest, pl.ds(c * (nx // 2), nx // 2), lax.rem(y + ny - b, ny)]
        sem = b * 2 + c
        return remote(there, there, by_send.at[sem], by_recv.at[sem], at_y(1))

    def relay_row(b):
        for c in range(2):
            row_came(b, c).wait_recv()
            step = onward(b, c, ny)
            if step:
                row(b, c, step).start()

    to_right = [0, *range(reach + 1, ny)]

    def spread(b):
        along_x(b, 0, right_send, right_recv, 1).start()
        along_x(b, 0, left_send, left_recv, nx - 1).start()

    def relay_y(b):
        landed_y(b).wait_recv()
        if b < reach:
            along_y(b, 1).start()
        elif b > reach + 1:
            along_y(b, ny - 1).start()
        spread(b)

    def relay_x(b):
        if b in to_right:
            along_x(b, nx - 1, right_send, right_recv, 1).wait_recv()
            along_x(b, nx - 1, pass_send, pass_recv, 1).start()
        else:
            along_x(b, 1, left_send, left_recv, nx - 1).wait_recv()
            along_x(b, 1, pass_send, pass_recv, nx - 1).start()

    with jax.named_scope("states_x"):
        xin[0] = loc[x]
        for copy in first:
            copy.wait_recv()
    tot[...] = sum(xin[d].astype(F32) for d in range(nx)).astype(BF16)
    second = [remote(tot, yin.at[d], y_send.at[d], y_recv.at[d], at_y(d)) for d in range(1, ny)]
    for copy in second:
        copy.start()

    with jax.named_scope("fetched"):
        wo[z, x, y] = wo_ref[mine, :]
        for d in range(1, nz):
            fetch(d, lax.rem(z + nz - d, nz)).wait_recv()
    along_y(0, 1).start()
    along_y(0, ny - 1).start()
    for d in range(1, nx):
        side(d).start()
    spread(0)
    for i in range(1, pieces):
        for step in (1, nz - 1):
            piece(0, i, step).start()

    positions = q_ref.shape[0]
    causal = lax.broadcasted_iota(jnp.int32, (positions, positions), 0) >= lax.broadcasted_iota(
        jnp.int32, (positions, positions), 1
    )

    def inner(begin, end):
        for i in range(begin, end):
            cols = slice(i * HD, (i + 1) * HD)
            scores = dot(q_ref[:, cols], k_ref[:, cols], ((1,), (1,)))
            scores = jnp.where(causal, scores, 0.0).astype(BF16)
            att[:, cols] = dot(scores, v_ref[:, cols])

    inner(0, heads // 2)
    with jax.named_scope("relay_1"):
        for d in range(1, nx):
            side_came(d).wait_recv()
        for c in range(2):
            for step in (1, ny - 1):
                row(0, c, step).start()
        relay_y(1)
        relay_y(ny - 1)
        relay_x(0)
        inner(heads // 2, heads)
        relay_row(1)
        relay_row(ny - 1)
        relay_y(2)
        relay_y(ny - 2)

    before = jnp.zeros(tot.shape, F32)
    with jax.named_scope("states_y"):
        for d in range(1, ny):
            second[d - 1].wait_recv()
            before = before + yin[d].astype(F32) * (d <= y).astype(F32)
    third = []
    for e in range(nx):
        target = lax.rem(x + e, nx)
        state = before
        for d in range(nx):
            source = lax.rem(x + nx - d, nx)
            state = state + xin[d].astype(F32) * (source < target).astype(F32)
        pre[e] = state.astype(BF16)
        if e:
            copy = remote(pre.at[e], pin.at[e], p_send.at[e], p_recv.at[e], at_x(e))
            copy.start()
            third.append(copy)
    pin[0] = pre[0]
    with jax.named_scope("relay_2"):
        for step in range(2, reach):
            if step > 2:
                relay_y(step)
                relay_y(ny - step)
            relay_row(step)
            relay_row(ny - step)
            relay_x(step - 1)
            relay_x(ny - step + 1)
            if step == 2:
                relay_ring(1, 0)
        relay_y(reach)
        relay_row(reach)
        relay_x(reach - 1)
        relay_x(reach + 1)
        relay_ring(1, 1)
    place(ids_ref, gates_ref, own_weighing)
    weighing[0] = own_weighing[y]
    shared = [
        remote(
            own_weighing.at[lax.rem(y + d, ny)], weighing.at[d], g_send.at[d], g_recv.at[d], at_y(d)
        )
        for d in range(1, ny)
    ]
    for copy in shared:
        copy.start()
    with jax.named_scope("mix"):
        for e in range(nx):
            if e:
                third[e - 1].wait_recv()
            for j in range(part):
                head = lax.rem(x + nx - e, nx) * part + j
                cols = rows(head, HD)
                state = (init_ref[head] + pin[e, j].astype(F32)).astype(BF16)
                out = att[:, cols] + dot(q_ref[:, cols], state)
                inv = lax.rsqrt(jnp.mean(out * out, axis=1, keepdims=True) + 1e-05)
                mixed[:, cols] = (out * inv * out_gain_ref[:, cols]).astype(BF16)
    with jax.named_scope("relay_3"):
        relay_x(reach)
        for b in range(ny):
            if b in to_right:
                along_x(b, 1, left_send, left_recv, nx - 1).wait_recv()
                along_x(b, 2, pass_send, pass_recv, 1).wait_recv()
            else:
                along_x(b, nx - 1, right_send, right_recv, 1).wait_recv()
                along_x(b, 2, pass_send, pass_recv, nx - 1).wait_recv()

    relay_ring(2, 0)
    halves = []
    for j in range(2):
        for c in range(j * nz // 2, (j + 1) * nz // 2):
            proj[:, c * width : (c + 1) * width] = dot(
                mixed[...], wo[c].reshape(nx * ny * depth, width)
            )
        cols = slice(j * HALF, (j + 1) * HALF)
        snd[j] = proj[rows(1 - h, tokens), cols].astype(BF16)
        halves.append(
            remote(snd.at[j], rcv.at[j], h_sem.at[j], h_sem.at[2 + j], (s, 1 - h, z))
        )
        halves[j].start()
    relay_ring(2, 1)
    for copy in first + second + third:
        copy.wait_send()
    for d in range(1, nz):
        fetch(d, z).wait_send()
    for b in range(ny):
        along_x(b, 0, right_send, right_recv, 1).wait_send()
        along_x(b, 0, left_send, left_recv, nx - 1).wait_send()
        if b in to_right:
            along_x(b, nx - 1, pass_send, pass_recv, 1).wait_send()
        else:
            along_x(b, 1, pass_send, pass_recv, nx - 1).wait_send()
        if b and b <= reach:
            along_y(b - 1, 1).wait_send()
        elif b:
            along_y((b + 1) % ny, ny - 1).wait_send()
        if b:
            for c in range(2):
                row_came(b, c).wait_send()
    for d in range(1, nx):
        side(d).wait_send()
    for half in halves:
        half.wait_recv()
    other = jnp.concatenate([rcv[0], rcv[1]], axis=1).astype(F32)
    stream = (
        res_ref[...].astype(F32) + (proj[rows(h, tokens), :] + other)
    ).astype(BF16)
    stream_ref[...] = stream
    stream_f = stream.astype(F32)
    inv = lax.rsqrt(jnp.mean(stream_f * stream_f, axis=1, keepdims=True) + 1e-06)
    moe_in = (stream_f * inv * gain_ref[...]).astype(BF16)
    chunks, wide = feats.shape[1], feats.shape[3]
    for c in range(chunks):
        feats[0, c, :tokens, :] = moe_in[:, c * wide : (c + 1) * wide]
        feats[0, c, tokens:, :] = moe_in[:, HALF + c * wide : HALF + (c + 1) * wide]

    def ring(b, c, step):
        arrives = (b + step) % ny
        sem = arrives * chunks + c
        return remote(
            feats.at[b, c], feats.at[arrives, c], f_send.at[sem], f_recv.at[sem], at_y(step)
        )

    for c in range(chunks):
        ring(0, c, 1).start()
        ring(0, c, ny - 1).start()
    for d in range(1, ny):
        shared[d - 1].wait_recv()

    def block(b, k):
        other = lax.rem(sub + k, across)
        slot = position((ny - b) % ny, ny) * across + sub
        sem = b * across + k
        return remote(
            outgoing.at[rows(b * across + other, BLK), :], incoming_ref.at[rows(slot, BLK), :],
            send.at[sem], recv.at[sem], at_sub(k),
        )

    def arrived(b, k):
        other = lax.rem(sub + across - k, across)
        slot = position((ny - b) % ny, ny) * across + other
        sem = b * across + k
        return remote(
            outgoing.at[rows(b * across + other, BLK), :], incoming_ref.at[rows(slot, BLK), :],
            send.at[sem], recv.at[sem], at_sub(k),
        )

    def keep(b):
        slot = position((ny - b) % ny, ny) * across + sub
        return pltpu.make_async_copy(
            outgoing.at[rows(b * across + sub, BLK), :], incoming_ref.at[rows(slot, BLK), :], own_sem.at[b]
        )

    group = across * BLK
    around = [0]
    for step in range(1, reach):
        around += [step, ny - step]
    around.append(reach)
    for b in around:
        if b == 2:
            relay_ring(3, 0)
        if b == reach:
            relay_ring(3, 1)
        picks = jnp.where(weighing[b].astype(F32) > 0.0, 1.0, 0.0).astype(BF16)
        for c in range(chunks):
            if b:
                step = way(b, c, ny)
                ring((b - step) % ny, c, step).wait_recv()
                step = onward(b, c, ny)
                if step:
                    ring(b, c, step).start()
            outgoing[b * group : (b + 1) * group, c * wide : (c + 1) * wide] = dot(
                picks, feats[b, c], ((0,), (0,))
            ).astype(BF16)

        def begin(k, carry, b=b):
            block(b, k).start()
            return carry

        lax.fori_loop(1, across, begin, 0)
        keep(b).start()

    for half in halves:
        half.wait_send()
    for copy in shared:
        copy.wait_send()
    for b in range(1, ny):
        for c in range(chunks):
            step = way(b, c, ny)
            ring((b - step) % ny, c, step).wait_send()
    for copy in kept:
        copy.wait()
    for b in around:
        keep(b).wait()

        def finish(k, carry, b=b):
            block(b, k).wait_send()
            arrived(b, k).wait_recv()
            return carry

        lax.fori_loop(1, across, finish, 0)

    def last():
        for later in range(2):
            relay_ring(nz // 2, later)

    run_experts(
        nx, ny, nz, last, incoming_ref, gate_full_ref, up_full_ref, down_full_ref, stream_ref, weighing, out_ref, *for_experts
    )
    for b in range(1, nz):
        for i in range(pieces):
            piece_came(b, i).wait_send()


def in_vmem(n):
    return [pl.BlockSpec(memory_space=pltpu.VMEM)] * n


def shards(
    nx, ny,
    query_proj, key_proj, value_proj, init_state, residual, out_gain, proj_weight, moe_gain,
    w_gate, w_up, w_down, expert_ids, gate_weights,
):
    tok, width = query_proj.shape[1:]
    heads = width // HD
    part = heads // nx
    token_rows = residual.shape[1]
    count = nx * ny * 2
    slots = count * BLK
    group = 2 * nx * BLK

    state = (part, HD, HD)
    nz = lax.axis_size("expert")
    depth, shard = proj_weight.shape
    dma = pltpu.SemaphoreType.DMA
    passing = (CHUNKS, 2 * token_rows, HALF // CHUNKS)
    out = pl.pallas_call(
        functools.partial(layer_kernel, nx, ny, nz),
        out_shape=jax.ShapeDtypeStruct((token_rows, D), BF16),
        in_specs=[*in_vmem(10), *[pl.BlockSpec(memory_space=pl.ANY)] * 3],
        out_specs=pl.BlockSpec(memory_space=pltpu.VMEM),
        scratch_shapes=[
            pltpu.VMEM((token_rows, D), BF16),
            pltpu.VMEM((slots, HALF), BF16),
            *[pltpu.VMEM((nz, *w_down.shape[1:]), BF16)] * 3,
            pltpu.VMEM((nx, *state), BF16),
            pltpu.VMEM((nx, *state), BF16),
            pltpu.VMEM(state, BF16),
            pltpu.VMEM((ny, *state), BF16),
            pltpu.VMEM((nx, *state), BF16),
            pltpu.VMEM((nx, *state), BF16),
            pltpu.VMEM((tok, width), F32),
            pltpu.VMEM((tok, width), BF16),
            pltpu.VMEM((nz, nx, ny, depth // (nx * ny), shard), BF16),
            pltpu.VMEM((tok, D), F32),
            pltpu.VMEM((2, token_rows, HALF), BF16),
            pltpu.VMEM((2, token_rows, HALF), BF16),
            pltpu.VMEM((ny, 2 * token_rows, group), BF16),
            pltpu.VMEM((ny, 2 * token_rows, group), BF16),
            pltpu.VMEM((ny, CHUNKS, 2 * token_rows, HALF // CHUNKS), BF16),
            pltpu.VMEM((slots, HALF), BF16),
            *[dma((n,)) for n in (nx, nx, ny, ny, nx, nx, nz, nz, ny, ny, ny, ny, ny, ny, ny, ny, 4)],
            *[dma((n,)) for n in (ny, ny, ny, ny * CHUNKS, ny * CHUNKS, count, count)],
            *[dma((n,)) for n in (nx, nx, 2 * ny, 2 * ny, 6 * nz, 6 * nz, 3)],
            pltpu.VMEM((slots, HALF), BF16),
            pltpu.VMEM((slots, HALF), BF16),
            *[pltpu.VMEM((n, *passing), BF16) for n in [ny // 2] * 4],
            *[dma((n,)) for n in (count, count)],
            *[dma((n * CHUNKS,)) for n in [ny // 2] * 4],
            pltpu.VMEM((nz, count * CAP, D // nz), BF16),
            pltpu.VMEM((2, count * CAP, w_down.shape[1]), F32),
        ],
        compiler_params=pltpu.CompilerParams(
            collective_id=0, has_side_effects=True, vmem_limit_bytes=VMEM_LIMIT
        ),
        cost_estimate=pl.CostEstimate(flops=10**9, bytes_accessed=3 * 10**8, transcendentals=0),
        name="layer",
    )(
        query_proj[0], key_proj[0], value_proj[0], init_state[0], out_gain[None, :], proj_weight,
        residual[0], moe_gain[None, :], expert_ids.transpose(2, 0, 1), gate_weights.transpose(2, 0, 1), w_gate[0], w_up[0], w_down[0],
    )
    return out[None]


def solution(mesh):
    placed = (
        P("expert", "seq", "head"),
        P("expert", "seq", "head"),
        P("expert", "seq", "head"),
        P("expert", "head", None, None),
        P("expert", ("seq", "head"), None),
        P("head"),
        P("head", "expert"),
        P(),
        P(("seq", "head"), None, "expert"),
        P(("seq", "head"), None, "expert"),
        P(("seq", "head"), None, "expert"),
        P("expert", ("seq", "head"), None),
        P("expert", ("seq", "head"), None),
    )
    nx, ny = grid_of(mesh.shape["seq"])
    return jax.shard_map(
        functools.partial(shards, nx, ny),
        mesh=mesh,
        in_specs=placed,
        out_specs=P("expert", ("seq", "head"), None),
        check_vma=False,
    )
```
